256 devices in a mesh: rows: 64 (over z, y, core), cols: 4 (over x).
Axes of the slice: x: 4, y: 4, z: 8, core: 2. Of those that a mesh axis runs over, the one named last changes fastest.
Arguments:
- crawl: bfloat16 [65536, 128], P('rows'), may hold values from -16 to 16
- bench: bfloat16 [16384, 128], P('cols'), may hold values from -2 to 2
- start_duals: float32 [16384], P('cols'), may hold values from -0.15 to 0.15
- row_cotangent: float32 [65536], P('rows'), may hold values from -24 to 24
- col_cotangent: float32 [16384], P('cols'), may hold values from -24 to 24
Outputs:
- crawl_grad: float32 [65536, 128], P('rows')
- bench_grad: float32 [16384, 128], P('cols')
The draws below stay inside these ranges and needn't reach their ends.
All inputs are finite; a program needn't handle non-finite values.
Results may differ from the reference program's by a relative error of at most 0.0039.
Values sent between devices are 32-bit elements; how exact they have to be, the bound alone decides.
A program may use at most 64 MiB of HBM per device.

```python
import math
import jax
import jax.numpy as jnp
from jax import lax

D = 128
N = 65536
M = 16384


def lowered_columns(key):
    marks = jax.random.randint(jax.random.fold_in(key, 7), (M,), 0, 64)
    return (marks == 0) & (jnp.roll(marks, 1) != 0)


def bench_parts(key, spread, shrink):
    normal = jax.random.normal(jax.random.fold_in(key, 5), (M, D), jnp.float32)
    factor = jnp.exp(spread * jax.random.uniform(jax.random.fold_in(key, 6), (M, 1), jnp.float32, -1.0, 1.0))
    lowered = lowered_columns(key)
    scale = factor * jnp.where(lowered[:, None], shrink, 1.0)
    return (normal, scale)


def draw_bench(key, part):
    normal, scale = bench_parts(key, 0.0, 1.0)
    return (0.12 * normal * scale).astype(jnp.bfloat16)


def draw_crawl(key, part):
    key = jax.random.fold_in(key, 1)
    values = 0.12 * jax.random.normal(key, (N, D), jnp.float32)
    return values.astype(jnp.bfloat16)


def steps_of(rng, extent, pieces, low, largest):
    loudness = 1.0
    for axis_at, parts in pieces:
        steps = jax.random.uniform(jax.random.fold_in(jax.random.fold_in(rng, 6), axis_at), (parts,), jnp.float32, low / len(pieces), largest / len(pieces))
        loudness = loudness * jnp.repeat(jnp.exp(steps), extent[axis_at] // parts).reshape((-1,) + (1,) * (len(extent) - 1 - axis_at))
    return loudness


def scatter_about(own_key, shape, scale, bound, shards=(), kind=jnp.bfloat16):
    result = jax.random.normal(own_key, shape, jnp.float32) * scale
    if len(shards) > 0:
        result = steps_of(own_key, shape, shards, -0.22, 0.18) * result
    return jnp.clip(result, min=-bound, max=bound).astype(kind)


def setup_inputs(seed: int = 0) -> dict:
    key_list = jax.random.split(jax.random.key(seed), 6)
    return {
        "crawl": draw_crawl(jax.random.fold_in(key_list[5], 71), 0),
        "bench": draw_bench(jax.random.fold_in(key_list[5], 71), 0),
        "start_duals": jnp.clip(jax.random.uniform(key_list[2], (M,), jnp.float32, -0.15, 0.15) * steps_of(key_list[2], (M,), ((0, 4),), -0.4, 0.0), -0.15, 0.15),
        "row_cotangent": scatter_about(key_list[3], (N,), 4.0, 24.0, ((0, 64),), jnp.float32),
        "col_cotangent": scatter_about(key_list[4], (M,), 4.0, 24.0, ((0, 4),), jnp.float32),
    }


EPSILON = 0.05


def reference(crawl, bench, start_duals, row_cotangent, col_cotangent):
    block_rows = math.gcd(N, 1024)
    block_count = N // block_rows
    crawl_blocks = crawl.reshape(block_count, block_rows, D)
    log_bench = math.log(M)
    log_crawl = math.log(N)

    def scores(crawl_block):
        return lax.dot_general(crawl_block, bench, (((1,), (1,)), ((), ())), preferred_element_type=jnp.float32)

    def row_lse(col_duals):
        def block_levels(crawl_block):
            logits = (col_duals[None, :] + scores(crawl_block)) / EPSILON
            highest = jnp.max(logits, 1)
            return highest + jnp.log(jnp.sum(jnp.exp(logits - highest[:, None]), 1))
        return lax.map(block_levels, crawl_blocks).reshape(N)

    def col_lse(row_duals):
        dual_blocks = row_duals.reshape(block_count, block_rows)

        def peak(running, element):
            logits = (element[1][:, None] + scores(element[0])) / EPSILON
            return jnp.maximum(running, jnp.max(logits, 0)), None

        highest, _ = lax.scan(peak, jnp.full((M,), -jnp.inf, jnp.float32), (crawl_blocks, dual_blocks))

        def accumulate(running, element):
            logits = (element[1][:, None] + scores(element[0])) / EPSILON
            return running + jnp.sum(jnp.exp(logits - highest[None, :]), 0), None

        summed, _ = lax.scan(accumulate, jnp.zeros((M,), jnp.float32), (crawl_blocks, dual_blocks))
        return highest + jnp.log(summed)

    row_level1 = row_lse(start_duals)
    row_dual1 = -EPSILON * (row_level1 - log_bench)
    col_level1 = col_lse(row_dual1)
    col_dual1 = -EPSILON * (col_level1 - log_crawl)
    row_level2 = row_lse(col_dual1)
    row_dual2 = -EPSILON * (row_level2 - log_bench)
    col_level2 = col_lse(row_dual2)

    def split(vector):
        return vector.reshape(block_count, block_rows)

    def first_pass(running, element):
        crawl_block, dual_block, level_block, cot_block = element
        tile = scores(crawl_block)
        col_soft2 = jnp.exp((dual_block[:, None] + tile) / EPSILON - col_level2[None, :])
        row_back2 = cot_block - jnp.sum(col_soft2 * col_cotangent[None, :], 1)
        row_soft2 = jnp.exp((col_dual1[None, :] + tile) / EPSILON - level_block[:, None])
        return running - jnp.sum(row_soft2 * row_back2[:, None], 0), row_back2

    col_back1, row_back2 = lax.scan(first_pass, jnp.zeros((M,), jnp.float32),
                                    (crawl_blocks, split(row_dual2), split(row_level2), split(row_cotangent)))

    def second_pass(element):
        crawl_block, dual_block = element
        col_soft1 = jnp.exp((dual_block[:, None] + scores(crawl_block)) / EPSILON - col_level1[None, :])
        return -jnp.sum(col_soft1 * col_back1[None, :], 1)

    row_back1 = lax.map(second_pass, (crawl_blocks, split(row_dual1)))

    def third_pass(running, element):
        crawl_block, dual1, dual2, level1, level2, back1, back2 = element
        tile = scores(crawl_block)
        col_soft2 = jnp.exp((dual2[:, None] + tile) / EPSILON - col_level2[None, :])
        row_soft2 = jnp.exp((col_dual1[None, :] + tile) / EPSILON - level2[:, None])
        col_soft1 = jnp.exp((dual1[:, None] + tile) / EPSILON - col_level1[None, :])
        row_soft1 = jnp.exp((start_duals[None, :] + tile) / EPSILON - level1[:, None])
        score_grad = -(col_soft2 * col_cotangent[None, :] + row_soft2 * back2[:, None]
                       + col_soft1 * col_back1[None, :] + row_soft1 * back1[:, None])
        score_grad = score_grad.astype(jnp.bfloat16)
        crawl_part = jnp.dot(score_grad, bench, preferred_element_type=jnp.float32)
        bench_part = lax.dot_general(score_grad, crawl_block, (((0,), (0,)), ((), ())), preferred_element_type=jnp.float32)
        return running + bench_part, crawl_part

    bench_grad, crawl_parts = lax.scan(third_pass, jnp.zeros((M, D), jnp.float32),
                                       (crawl_blocks, split(row_dual1), split(row_dual2), split(row_level1),
                                        split(row_level2), row_back1, row_back2))
    return crawl_parts.reshape(N, D), bench_grad
```

```python
import functools
import math

import jax
import jax.numpy as jnp
from jax import lax
from jax.experimental import pallas as pl
from jax.experimental.pallas import tpu as pltpu
from jax.sharding import PartitionSpec as P

EPSILON = 0.05
SCALE = math.log2(math.e) / EPSILON
MESH = pl.DeviceIdType.MESH
F32 = jnp.float32
CORES, YS = 2, 4


def kernel(
    nx, nz,
    crawl, bench, start, row_cot, col_cot,
    crawl_out, bench_out,
    tile, crawl_t, grads, lane_max, lane_sum, alpha_b, beta_b, back_b,
    rowvec, colmax, fvec, gvec, avec, bvec,
    xs1, xr1, xs, xr, as1, ar1, as_, ar, zs1, zr1, zs, zr, cg,
    crawl_acc, crawl_recv, bench_part, sib, ysend, yrecv, zpart, zrecv,
    x_ss, x_rs, a_ss, a_rs, z_ss, z_rs, g_ss, g_rs,
    cr_ss, cr_rs, ca_ss, ca_rs, sib_ss, sib_rs, y_ss, y_rs, fz_ss, fz_rs,
    gz_ss, gz_rs, gy_ss, gy_rs, gc_ss, gc_rs,
):
    rows, depth = crawl.shape
    cols = bench.shape[0]
    half, part = cols // CORES, cols // (CORES * YS)
    na = CORES * YS
    r, c = lax.axis_index("rows"), lax.axis_index("cols")
    k, y, z = lax.rem(r, CORES), lax.rem(lax.div(r, CORES), YS), lax.div(r, na)
    a = lax.rem(r, na)

    def at(k_, y_, z_):
        return ((z_ * YS + y_) * CORES + k_, c)

    x_peers = [(r, lax.rem(c + d, nx)) for d in range(1, nx)]
    a_peers = []
    for d in range(1, na):
        o = lax.rem(a + d, na)
        a_peers.append((lax.rem(o, CORES), at(lax.rem(o, CORES), lax.div(o, CORES), z)))
    z_peers = [(lax.rem(z + d, nz), at(k, y, lax.rem(z + d, nz))) for d in range(1, nz)]
    sibling = at(1 - k, y, z)

    barrier = pltpu.get_barrier_semaphore()
    everyone = x_peers + [p for _, p in a_peers] + [p for _, p in z_peers]
    for p in everyone:
        pl.semaphore_signal(barrier, inc=1, device_id=p, device_id_type=MESH)

    def send(src, dst, ss, rs, p):
        pltpu.make_async_remote_copy(
            src_ref=src, dst_ref=dst, send_sem=ss, recv_sem=rs, device_id=p, device_id_type=MESH
        ).start()

    def take(ref, sem):
        pltpu.make_async_copy(ref, ref, sem).wait()

    def x_exchange(n, src, recv):
        recv[c] = src[...]
        for p in x_peers:
            send(src, recv.at[c], x_ss.at[n], x_rs.at[n], p)
        others = recv.at[pl.ds(0, nx - 1)]
        take(others, x_rs.at[n])
        take(others, x_ss.at[n])

    def a_exchange(n, src, recv):
        recv[a] = src[k]
        for o, p in a_peers:
            send(src.at[o], recv.at[a], a_ss.at[n], a_rs.at[n], p)
        others = recv.at[pl.ds(0, na - 1)]
        take(others, a_rs.at[n])
        take(others, a_ss.at[n])

    def z_exchange(n, src, recv):
        recv[z] = src[...]
        for _, p in z_peers:
            send(src, recv.at[z], z_ss.at[n], z_rs.at[n], p)
        others = recv.at[pl.ds(0, nz - 1)]
        take(others, z_rs.at[n])
        take(others, z_ss.at[n])

    def core_gather(n, value):
        cg[n, k] = value
        send(cg.at[n, k], cg.at[n, k], g_ss.at[n], g_rs.at[n], sibling)
        take(cg.at[n, k], g_rs.at[n])
        take(cg.at[n, k], g_ss.at[n])

    def summed(recv, n):
        total = recv[0]
        for i in range(1, n):
            total = total + recv[i]
        return total

    def combined(recv, n):
        top = recv[0, 0:1, :]
        for i in range(1, n):
            top = jnp.maximum(top, recv[i, 0:1, :])
        total = recv[0, 1:2, :] * jnp.exp2(recv[0, 0:1, :] - top)
        for i in range(1, n):
            total = total + recv[i, 1:2, :] * jnp.exp2(recv[i, 0:1, :] - top)
        return top, total

    def spread(vec, out):
        for i in range(rows // 128):
            piece = vec[:, i * 128 : (i + 1) * 128]
            out[i * 128 : (i + 1) * 128, :] = jnp.broadcast_to(piece, (128, 128)).T

    def row_pass(d, out):
        def step(i, carry):
            base = pl.multiple_of(i * 128, 128)
            pieces = []
            for h in range(2):
                acc = jnp.zeros((64, 128), F32)
                for j in range(cols // 128):
                    s = slice(j * 128, (j + 1) * 128)
                    acc = acc + tile[pl.ds(base + h * 64, 64), s] * d[0:1, s]
                pieces.append(acc)
            acc = jnp.concatenate(pieces, 0).T
            out[0:1, pl.ds(base, 128)] = jnp.sum(acc, 0, keepdims=True)
            return carry

        lax.fori_loop(0, rows // 128, step, 0)

    width = min(1024, cols)

    def col_pass(w, finish):
        for cb in range(cols // width):
            def step(i, accs, cb=cb):
                base = pl.multiple_of(i * 64, 64)
                wb = w[pl.ds(base, 64), :]
                new = []
                for j in range(width // 128):
                    o = cb * width + j * 128
                    t = tile[pl.ds(base, 64), o : o + 128] * wb
                    new.append(accs[j] + jnp.sum(t.reshape(8, 8, 128), 0))
                return tuple(new)

            accs = lax.fori_loop(
                0, rows // 64, step, tuple(jnp.zeros((8, 128), F32) for _ in range(width // 128))
            )
            for j in range(width // 128):
                finish(cb * width + j * 128, jnp.sum(accs[j], 0, keepdims=True))

    crawl_t[...] = crawl[...].astype(F32).T.astype(jnp.bfloat16)
    lane_max[...] = jnp.full(lane_max.shape, -jnp.inf, F32)
    mm = min(512, cols)
    rb = min(256, rows)

    def score_step(t, carry):
        i, jb = lax.rem(t, rows // rb), lax.div(t, rows // rb)
        base = pl.multiple_of(i * rb, rb)
        off = pl.multiple_of(jb * mm, mm)
        s = lax.dot_general(
            crawl[pl.ds(base, rb), :], bench[pl.ds(off, mm), :], (((1,), (1,)), ((), ())),
            preferred_element_type=F32,
        )
        s = s * SCALE + start[0:1, pl.ds(off, mm)] * SCALE
        tile[pl.ds(base, rb), pl.ds(off, mm)] = s
        top = lane_max[pl.ds(base, rb), :]
        for j in range(mm // 128):
            top = jnp.maximum(top, s[:, j * 128 : (j + 1) * 128])
        lane_max[pl.ds(base, rb), :] = top
        return carry

    lax.fori_loop(0, (rows // rb) * (cols // mm), score_step, 0)

    def level_step(i, carry):
        base = pl.multiple_of(i * 128, 128)
        tops, sums = [], []
        for h in range(2):
            at_ = pl.ds(base + h * 64, 64)
            top = lane_max[at_, :]
            acc = jnp.zeros((64, 128), F32)
            for j in range(cols // 128):
                acc = acc + jnp.exp2(tile[at_, j * 128 : (j + 1) * 128] - top)
            tops.append(top)
            sums.append(acc)
        top = jnp.concatenate(tops, 0).T
        acc = jnp.concatenate(sums, 0).T
        best = jnp.max(top, 0, keepdims=True)
        xs1[0:1, pl.ds(base, 128)] = best
        xs1[1:2, pl.ds(base, 128)] = jnp.sum(acc * jnp.exp2(top - best), 0, keepdims=True)
        return carry

    lax.fori_loop(0, rows // 128, level_step, 0)
    pl.semaphore_wait(barrier, len(everyone))
    x_exchange(0, xs1, xr1)
    top, total = combined(xr1, nx)
    spread(top + jnp.log2(total), alpha_b)

    for cb in range(cols // width):
        def top_step(i, tops, cb=cb):
            base = pl.multiple_of(i * 64, 64)
            lev = alpha_b[pl.ds(base, 64), :]
            new = []
            for j in range(width // 128):
                o = cb * width + j * 128
                t = tile[pl.ds(base, 64), o : o + 128] - lev
                new.append(jnp.maximum(tops[j], jnp.max(t.reshape(8, 8, 128), 0)))
            return tuple(new)

        tops = lax.fori_loop(
            0, rows // 64, top_step, tuple(jnp.full((8, 128), -jnp.inf, F32) for _ in range(width // 128))
        )
        tops = [jnp.max(t, 0, keepdims=True) for t in tops]
        for j in range(width // 128):
            colmax[0:1, cb * width + j * 128 : cb * width + (j + 1) * 128] = tops[j]

        def exp_step(i, accs, cb=cb):
            base = pl.multiple_of(i * 64, 64)
            lev = alpha_b[pl.ds(base, 64), :]
            new = []
            for j in range(width // 128):
                o = cb * width + j * 128
                e = jnp.exp2((tile[pl.ds(base, 64), o : o + 128] - lev) - colmax[0:1, o : o + 128])
                tile[pl.ds(base, 64), o : o + 128] = e
                new.append(accs[j] + jnp.sum(e.reshape(8, 8, 128), 0))
            return tuple(new)

        accs = lax.fori_loop(
            0, rows // 64, exp_step, tuple(jnp.zeros((8, 128), F32) for _ in range(width // 128))
        )
        for j in range(width // 128):
            o = cb * width + j * 128
            h, p = o // half, o % half
            as1[h, 0:1, p : p + 128] = tops[j]
            as1[h, 1:2, p : p + 128] = jnp.sum(accs[j], 0, keepdims=True)
    gvec[...] = jnp.exp2(colmax[...])

    a_exchange(0, as1, ar1)
    top, total = combined(ar1, na)
    zs1[0:1, :] = top
    zs1[1:2, :] = total
    z_exchange(0, zs1, zr1)
    top, total = combined(zr1, nz)
    core_gather(0, top + jnp.log2(total))
    for h in range(CORES):
        s = slice(h * half, (h + 1) * half)
        fvec[0:1, s] = jnp.exp2(colmax[0:1, s] - cg[0, h])

    row_pass(fvec, xs.at[0])
    x_exchange(1, xs.at[0], xr.at[0])
    alpha = 1.0 / summed(xr.at[0], nx)
    rowvec[...] = alpha
    spread(alpha, alpha_b)

    def col_reduce(n, w):
        def finish(o, v):
            h, p = o // half, o % half
            as_[n, h, 0:1, p : p + 128] = v * fvec[0:1, o : o + 128]

        col_pass(w, finish)
        a_exchange(n + 1, as_.at[n], ar.at[n])
        zs[n] = summed(ar.at[n], na)
        z_exchange(n + 1, zs.at[n], zr.at[n])
        core_gather(n + 1, summed(zr.at[n], nz))

    col_reduce(0, alpha_b)
    for h in range(CORES):
        s = slice(h * half, (h + 1) * half)
        avec[0:1, s] = fvec[0:1, s] * col_cot[0:1, s] / cg[1, h]

    row_pass(avec, xs.at[1])
    x_exchange(2, xs.at[1], xr.at[1])
    back2 = row_cot[...] - rowvec[...] * summed(xr.at[1], nx)
    spread(back2 * rowvec[...], beta_b)

    col_reduce(1, beta_b)
    for h in range(CORES):
        s = slice(h * half, (h + 1) * half)
        bvec[0:1, s] = -fvec[0:1, s] * cg[2, h]

    row_pass(bvec, xs.at[2])
    x_exchange(3, xs.at[2], xr.at[2])
    spread(-summed(xr.at[2], nx), back_b)

    crawl_acc[...] = jnp.zeros(crawl_acc.shape, F32)

    def grad_chunk(off, out):
        def step(i, carry):
            base = pl.multiple_of(i * 64, 64)
            al, be, ba = (v[pl.ds(base, 64), :] for v in (alpha_b, beta_b, back_b))
            for j in range(part // 128):
                s = pl.ds(pl.multiple_of(off + j * 128, 128), 128)
                bracket = (al * avec[0:1, s] + be * fvec[0:1, s]) + (bvec[0:1, s] + ba * gvec[0:1, s])
                value = -(tile[pl.ds(base, 64), s] * bracket)
                grads[pl.ds(base, 64), j * 128 : (j + 1) * 128] = value.astype(jnp.bfloat16)
            return carry

        lax.fori_loop(0, rows // 64, step, 0)

        def product(i, carry):
            base = pl.multiple_of(i * rb, rb)
            crawl_acc[pl.ds(base, rb), :] += jnp.dot(
                grads[pl.ds(base, rb), :], bench[pl.ds(off, part), :], preferred_element_type=F32
            )
            return carry

        lax.fori_loop(0, rows // rb, product, 0)
        out[...] = jnp.dot(crawl_t[...], grads[...], preferred_element_type=F32)

    def ordered(s):
        return lax.rem(y + (2, 1, 3, 0)[s], YS)

    for s in range(YS):
        owner = ordered(s)
        theirs = pl.multiple_of((1 - k) * half + owner * part, part)
        mine = pl.multiple_of(k * half + owner * part, part)
        grad_chunk(theirs, bench_part.at[s])
        send(bench_part.at[s], sib.at[s], sib_ss.at[s], sib_rs.at[s], sibling)
        grad_chunk(mine, ysend.at[s])
        take(sib.at[s], sib_rs.at[s])
        if s < YS - 1:
            ysend[s] = ysend[s] + sib[s]
            send(ysend.at[s], yrecv.at[y], y_ss.at[s], y_rs, at(k, owner, z))
        else:
            yrecv[y] = ysend[s] + sib[s]

    quarter = rows // nx
    mine_rows = pl.ds(pl.multiple_of(c * quarter, quarter), quarter)
    for d, p in enumerate(x_peers):
        there = pl.ds(pl.multiple_of(p[1] * quarter, quarter), quarter)
        send(crawl_acc.at[there, :], crawl_recv.at[c], cr_ss.at[d], cr_rs, p)
    crawl_recv[c] = crawl_acc[mine_rows, :]

    others = yrecv.at[pl.ds(0, YS - 1)]
    take(others, y_rs)
    piece = part // nz
    for j in range(part // 128):
        s = slice(j * 128, (j + 1) * 128)
        total = yrecv[0, :, s]
        for i in range(1, YS):
            total = total + yrecv[i, :, s]
        zpart[s, :] = total.T
    for d, (o, p) in enumerate(z_peers):
        send(zpart.at[pl.ds(pl.multiple_of(o * piece, piece), piece), :], zrecv.at[z], fz_ss.at[d], fz_rs, p)
    zrecv[z] = zpart[pl.ds(pl.multiple_of(z * piece, piece), piece), :]

    take(crawl_recv.at[pl.ds(0, nx - 1)], cr_rs)
    crawl_out[mine_rows, :] = summed(crawl_recv, nx)
    for d, p in enumerate(x_peers):
        send(crawl_out.at[mine_rows, :], crawl_out.at[mine_rows, :], ca_ss.at[d], ca_rs, p)

    take(zrecv.at[pl.ds(0, nz - 1)], fz_rs)
    block = pl.multiple_of(k * half + y * part, part)
    own = pl.ds(pl.multiple_of(block + z * piece, piece), piece)
    bench_out[own, :] = summed(zrecv, nz)
    for d, (_, p) in enumerate(z_peers):
        send(bench_out.at[own, :], bench_out.at[own, :], gz_ss.at[d], gz_rs, p)
    take(zrecv.at[pl.ds(0, nz - 1)], gz_rs)
    mine_block = pl.ds(block, part)
    for s in range(YS - 1):
        send(bench_out.at[mine_block, :], bench_out.at[mine_block, :], gy_ss.at[s], gy_rs.at[s], at(k, ordered(s), z))
    send(bench_out.at[mine_block, :], bench_out.at[mine_block, :], gc_ss.at[YS - 1], gc_rs.at[YS - 1], sibling)
    for s in range(YS - 1):
        source = lax.rem(y + YS - (2, 1, 3)[s], YS)
        theirs = pl.ds(pl.multiple_of(k * half + source * part, part), part)
        take(bench_out.at[theirs, :], gy_rs.at[s])
        send(bench_out.at[theirs, :], bench_out.at[theirs, :], gc_ss.at[s], gc_rs.at[s], sibling)
    for s in range(YS):
        take(sib.at[s], gc_rs.at[s])
        take(sib.at[s], gc_ss.at[s])
        take(sib.at[s], sib_ss.at[s])
    for s in range(YS - 1):
        take(sib.at[s], gy_ss.at[s])
        take(sib.at[s], y_ss.at[s])
    for d in range(nz - 1):
        take(zrecv.at[0], fz_ss.at[d])
        take(zrecv.at[0], gz_ss.at[d])
    take(crawl_recv.at[pl.ds(0, nx - 1)], ca_rs)
    for d in range(nx - 1):
        take(crawl_recv.at[0], ca_ss.at[d])
        take(crawl_recv.at[0], cr_ss.at[d])


def solution(mesh):
    nx = mesh.shape["cols"]
    nz = mesh.shape["rows"] // (CORES * YS)
    na = CORES * YS

    def per_device(crawl, bench, start_duals, row_cotangent, col_cotangent):
        rows, depth = crawl.shape
        cols = bench.shape[0]
        half, part = cols // CORES, cols // (CORES * YS)
        vmem, dma = pltpu.VMEM, pltpu.SemaphoreType.DMA
        scratch = [
            vmem((rows, cols), F32),
            vmem((depth, rows), jnp.bfloat16),
            vmem((rows, part), jnp.bfloat16),
            vmem((rows, 128), F32),
            vmem((rows, 128), F32),
            vmem((rows, 128), F32),
            vmem((rows, 128), F32),
            vmem((rows, 128), F32),
            vmem((1, rows), F32),
            *[vmem((1, cols), F32)] * 5,
            vmem((2, rows), F32), vmem((nx, 2, rows), F32),
            vmem((3, 1, rows), F32), vmem((3, nx, 1, rows), F32),
            vmem((CORES, 2, half), F32), vmem((na, 2, half), F32),
            vmem((2, CORES, 1, half), F32), vmem((2, na, 1, half), F32),
            vmem((2, half), F32), vmem((nz, 2, half), F32),
            vmem((2, 1, half), F32), vmem((2, nz, 1, half), F32),
            vmem((3, CORES, 1, half), F32),
            vmem((rows, depth), F32), vmem((nx, rows // nx, depth), F32),
            vmem((YS, depth, part), F32), vmem((YS, depth, part), F32),
            vmem((YS, depth, part), F32), vmem((YS, depth, part), F32),
            vmem((part, depth), F32), vmem((nz, part // nz, depth), F32),
            dma((4,)), dma((4,)), dma((3,)), dma((3,)), dma((3,)), dma((3,)), dma((3,)), dma((3,)),
            dma((nx - 1,)), dma, dma((nx - 1,)), dma,
            dma((YS,)), dma((YS,)), dma((YS - 1,)), dma, dma((nz - 1,)), dma,
            dma((nz - 1,)), dma, dma((YS - 1,)), dma((YS - 1,)), dma((YS,)), dma((YS,)),
        ]
        return pl.pallas_call(
            functools.partial(kernel, nx, nz),
            out_shape=(jax.ShapeDtypeStruct((rows, depth), F32), jax.ShapeDtypeStruct((cols, depth), F32)),
            in_specs=[pl.BlockSpec(memory_space=vmem)] * 5,
            out_specs=(pl.BlockSpec(memory_space=vmem),) * 2,
            scratch_shapes=scratch,
            compiler_params=pltpu.CompilerParams(
                collective_id=0, has_side_effects=True, vmem_limit_bytes=56 << 20
            ),
        )(crawl, bench, start_duals[None, :], row_cotangent[None, :], col_cotangent[None, :])

    placed = (P("rows", None), P("cols", None), P("cols"), P("rows"), P("cols"))
    return jax.shard_map(
        per_device,
        mesh=mesh,
        in_specs=placed,
        out_specs=(P("rows", None), P("cols", None)),
        check_vma=False,
    )
```

```python
import functools
import math

import jax
import jax.numpy as jnp
from jax import lax
from jax.experimental import pallas as pl
from jax.experimental.pallas import tpu as pltpu
from jax.sharding import PartitionSpec as P

EPSILON = 0.05
SCALE = math.log2(math.e) / EPSILON
MESH = pl.DeviceIdType.MESH
F32 = jnp.float32
CORES, YS = 2, 4


def kernel(
    nx, nz,
    crawl, bench, start, row_cot, col_cot,
    crawl_out, bench_out,
    tile, crawl_t, lane_max, alpha_b, beta_b, back_b,
    rowvec, colmax, fvec, gvec, avec, bvec,
    xs1, xr1, xs, xr, as1, ar1, as_, ar, zs1, zr1, zs, zr, cg,
    crawl_acc, crawl_recv, bench_part, sib, ysend, yrecv, zpart, zrecv,
    x_ss, x_rs, a_ss, a_rs, z_ss, z_rs, g_ss, g_rs,
    cr_ss, cr_rs, ca_ss, ca_rs, sib_ss, sib_rs, y_ss, y_rs, fz_ss, fz_rs,
    gz_ss, gz_rs, gy_ss, gy_rs, gc_ss, gc_rs,
):
    rows, depth = crawl.shape
    cols = bench.shape[0]
    half, part = cols // CORES, cols // (CORES * YS)
    na = CORES * YS
    r, c = lax.axis_index("rows"), lax.axis_index("cols")
    k, y, z = lax.rem(r, CORES), lax.rem(lax.div(r, CORES), YS), lax.div(r, na)
    a = lax.rem(r, na)

    def at(k_, y_, z_):
        return ((z_ * YS + y_) * CORES + k_, c)

    x_peers = [(r, lax.rem(c + d, nx)) for d in range(1, nx)]
    a_peers = []
    for d in range(1, na):
        o = lax.rem(a + d, na)
        a_peers.append((lax.rem(o, CORES), at(lax.rem(o, CORES), lax.div(o, CORES), z)))
    z_peers = [(lax.rem(z + d, nz), at(k, y, lax.rem(z + d, nz))) for d in range(1, nz)]
    sibling = at(1 - k, y, z)

    barrier = pltpu.get_barrier_semaphore()
    everyone = x_peers + [p for _, p in a_peers] + [p for _, p in z_peers]
    for p in everyone:
        pl.semaphore_signal(barrier, inc=1, device_id=p, device_id_type=MESH)

    def send(src, dst, ss, rs, p):
        pltpu.make_async_remote_copy(
            src_ref=src, dst_ref=dst, send_sem=ss, recv_sem=rs, device_id=p, device_id_type=MESH
        ).start()

    def take(ref, sem):
        pltpu.make_async_copy(ref, ref, sem).wait()

    def x_exchange(n, src, recv):
        recv[c] = src[...]
        for p in x_peers:
            send(src, recv.at[c], x_ss.at[n], x_rs.at[n], p)
        others = recv.at[pl.ds(0, nx - 1)]
        take(others, x_rs.at[n])
        take(others, x_ss.at[n])

    def a_exchange(n, src, recv):
        recv[a] = src[k]
        for o, p in a_peers:
            send(src.at[o], recv.at[a], a_ss.at[n], a_rs.at[n], p)
        others = recv.at[pl.ds(0, na - 1)]
        take(others, a_rs.at[n])
        take(others, a_ss.at[n])

    def z_exchange(n, src, recv):
        recv[z] = src[...]
        for _, p in z_peers:
            send(src, recv.at[z], z_ss.at[n], z_rs.at[n], p)
        others = recv.at[pl.ds(0, nz - 1)]
        take(others, z_rs.at[n])
        take(others, z_ss.at[n])

    def core_gather(n, value):
        cg[n, k] = value
        send(cg.at[n, k], cg.at[n, k], g_ss.at[n], g_rs.at[n], sibling)
        take(cg.at[n, k], g_rs.at[n])
        take(cg.at[n, k], g_ss.at[n])

    def summed(recv, n):
        total = recv[0]
        for i in range(1, n):
            total = total + recv[i]
        return total

    def combined(recv, n):
        top = recv[0, 0:1, :]
        for i in range(1, n):
            top = jnp.maximum(top, recv[i, 0:1, :])
        total = recv[0, 1:2, :] * jnp.exp2(recv[0, 0:1, :] - top)
        for i in range(1, n):
            total = total + recv[i, 1:2, :] * jnp.exp2(recv[i, 0:1, :] - top)
        return top, total

    def spread(vec, out):
        for i in range(rows // 128):
            piece = vec[:, i * 128 : (i + 1) * 128]
            out[i * 128 : (i + 1) * 128, :] = jnp.broadcast_to(piece, (128, 128)).T

    def row_pass(d, out):
        def step(i, carry):
            base = pl.multiple_of(i * 128, 128)
            pieces = []
            for h in range(2):
                acc = jnp.zeros((64, 128), F32)
                for j in range(cols // 128):
                    s = slice(j * 128, (j + 1) * 128)
                    acc = acc + tile[pl.ds(base + h * 64, 64), s] * d[0:1, s]
                pieces.append(acc)
            acc = jnp.concatenate(pieces, 0).T
            out[0:1, pl.ds(base, 128)] = jnp.sum(acc, 0, keepdims=True)
            return carry

        lax.fori_loop(0, rows // 128, step, 0)

    width = min(1024, cols)

    def col_pass(w, finish):
        for cb in range(cols // width):
            def step(i, accs, cb=cb):
                base = pl.multiple_of(i * 64, 64)
                wb = w[pl.ds(base, 64), :]
                new = []
                for j in range(width // 128):
                    o = cb * width + j * 128
                    t = tile[pl.ds(base, 64), o : o + 128] * wb
                    new.append(accs[j] + jnp.sum(t.reshape(8, 8, 128), 0))
                return tuple(new)

            accs = lax.fori_loop(
                0, rows // 64, step, tuple(jnp.zeros((8, 128), F32) for _ in range(width // 128))
            )
            for j in range(width // 128):
                finish(cb * width + j * 128, jnp.sum(accs[j], 0, keepdims=True))

    crawl_t[...] = crawl[...].astype(F32).T.astype(jnp.bfloat16)
    lane_max[...] = jnp.full(lane_max.shape, -jnp.inf, F32)
    mm = min(512, cols)
    rb = min(256, rows)

    def score_step(t, carry):
        i, jb = lax.rem(t, rows // rb), lax.div(t, rows // rb)
        base = pl.multiple_of(i * rb, rb)
        off = pl.multiple_of(jb * mm, mm)
        s = lax.dot_general(
            crawl[pl.ds(base, rb), :], bench[pl.ds(off, mm), :], (((1,), (1,)), ((), ())),
            preferred_element_type=F32,
        )
        s = s * SCALE + start[0:1, pl.ds(off, mm)] * SCALE
        tile[pl.ds(base, rb), pl.ds(off, mm)] = s
        top = lane_max[pl.ds(base, rb), :]
        for j in range(mm // 128):
            top = jnp.maximum(top, s[:, j * 128 : (j + 1) * 128])
        lane_max[pl.ds(base, rb), :] = top
        return carry

    lax.fori_loop(0, (rows // rb) * (cols // mm), score_step, 0, unroll=4)

    def level_step(i, carry):
        base = pl.multiple_of(i * 128, 128)
        tops, sums = [], []
        for h in range(2):
            at_ = pl.ds(base + h * 64, 64)
            top = lane_max[at_, :]
            acc = jnp.zeros((64, 128), F32)
            for j in range(cols // 128):
                acc = acc + jnp.exp2(tile[at_, j * 128 : (j + 1) * 128] - top)
            tops.append(top)
            sums.append(acc)
        top = jnp.concatenate(tops, 0).T
        acc = jnp.concatenate(sums, 0).T
        best = jnp.max(top, 0, keepdims=True)
        xs1[0:1, pl.ds(base, 128)] = best
        xs1[1:2, pl.ds(base, 128)] = jnp.sum(acc * jnp.exp2(top - best), 0, keepdims=True)
        return carry

    lax.fori_loop(0, rows // 128, level_step, 0)
    pl.semaphore_wait(barrier, len(everyone))
    x_exchange(0, xs1, xr1)
    top, total = combined(xr1, nx)
    spread(top + jnp.log2(total), alpha_b)

    for cb in range(cols // width):
        def top_step(i, tops, cb=cb):
            base = pl.multiple_of(i * 64, 64)
            lev = alpha_b[pl.ds(base, 64), :]
            new = []
            for j in range(width // 128):
                o = cb * width + j * 128
                t = tile[pl.ds(base, 64), o : o + 128] - lev
                new.append(jnp.maximum(tops[j], jnp.max(t.reshape(8, 8, 128), 0)))
            return tuple(new)

        tops = lax.fori_loop(
            0, rows // 64, top_step, tuple(jnp.full((8, 128), -jnp.inf, F32) for _ in range(width // 128))
        )
        tops = [jnp.max(t, 0, keepdims=True) for t in tops]
        for j in range(width // 128):
            colmax[0:1, cb * width + j * 128 : cb * width + (j + 1) * 128] = tops[j]

        def exp_step(i, accs, cb=cb):
            base = pl.multiple_of(i * 64, 64)
            lev = alpha_b[pl.ds(base, 64), :]
            new = []
            for j in range(width // 128):
                o = cb * width + j * 128
                e = jnp.exp2((tile[pl.ds(base, 64), o : o + 128] - lev) - colmax[0:1, o : o + 128])
                tile[pl.ds(base, 64), o : o + 128] = e
                new.append(accs[j] + jnp.sum(e.reshape(8, 8, 128), 0))
            return tuple(new)

        accs = lax.fori_loop(
            0, rows // 64, exp_step, tuple(jnp.zeros((8, 128), F32) for _ in range(width // 128))
        )
        for j in range(width // 128):
            o = cb * width + j * 128
            h, p = o // half, o % half
            as1[h, 0:1, p : p + 128] = tops[j]
            as1[h, 1:2, p : p + 128] = jnp.sum(accs[j], 0, keepdims=True)
    gvec[...] = jnp.exp2(colmax[...])

    a_exchange(0, as1, ar1)
    top, total = combined(ar1, na)
    zs1[0:1, :] = top
    zs1[1:2, :] = total
    z_exchange(0, zs1, zr1)
    top, total = combined(zr1, nz)
    core_gather(0, top + jnp.log2(total))
    for h in range(CORES):
        s = slice(h * half, (h + 1) * half)
        fvec[0:1, s] = jnp.exp2(colmax[0:1, s] - cg[0, h])

    row_pass(fvec, xs.at[0])
    x_exchange(1, xs.at[0], xr.at[0])
    alpha = 1.0 / summed(xr.at[0], nx)
    rowvec[...] = alpha
    spread(alpha, alpha_b)

    def col_reduce(n, w):
        def finish(o, v):
            h, p = o // half, o % half
            as_[n, h, 0:1, p : p + 128] = v * fvec[0:1, o : o + 128]

        col_pass(w, finish)
        a_exchange(n + 1, as_.at[n], ar.at[n])
        zs[n] = summed(ar.at[n], na)
        z_exchange(n + 1, zs.at[n], zr.at[n])
        core_gather(n + 1, summed(zr.at[n], nz))

    col_reduce(0, alpha_b)
    for h in range(CORES):
        s = slice(h * half, (h + 1) * half)
        avec[0:1, s] = fvec[0:1, s] * col_cot[0:1, s] / cg[1, h]

    row_pass(avec, xs.at[1])
    x_exchange(2, xs.at[1], xr.at[1])
    back2 = row_cot[...] - rowvec[...] * summed(xr.at[1], nx)
    spread(back2 * rowvec[...], beta_b)

    col_reduce(1, beta_b)
    for h in range(CORES):
        s = slice(h * half, (h + 1) * half)
        bvec[0:1, s] = -fvec[0:1, s] * cg[2, h]

    row_pass(bvec, xs.at[2])
    x_exchange(3, xs.at[2], xr.at[2])
    spread(-summed(xr.at[2], nx), back_b)

    crawl_acc[...] = jnp.zeros(crawl_acc.shape, F32)

    def grad_chunk(core, q, out):
        offs = [pl.multiple_of(core * half + o * part + q * 128, 128) for o in range(YS)]
        some_bench = jnp.concatenate([bench[pl.ds(o, 128), :] for o in offs], 0)
        acc = None
        for i in range(rows // rb):
            blocks = []
            for h in range(rb // 64):
                at_ = slice(i * rb + h * 64, i * rb + (h + 1) * 64)
                al, be, ba = alpha_b[at_, :], beta_b[at_, :], back_b[at_, :]
                pieces = []
                for o in offs:
                    s = pl.ds(o, 128)
                    bracket = (al * avec[0:1, s] + be * fvec[0:1, s]) + (bvec[0:1, s] + ba * gvec[0:1, s])
                    pieces.append((-(tile[at_, s] * bracket)).astype(jnp.bfloat16))
                blocks.append(jnp.concatenate(pieces, 1))
            grads = jnp.concatenate(blocks, 0)
            at_ = slice(i * rb, (i + 1) * rb)
            crawl_acc[at_, :] += jnp.dot(grads, some_bench, preferred_element_type=F32)
            product = jnp.dot(crawl_t[:, at_], grads, preferred_element_type=F32)
            acc = product if acc is None else acc + product
        out[...] = acc

    piece = part // nz
    quarters = part // 128
    per = nz // quarters

    def quarter(t):
        u = quarters - 1 - t
        if quarters == 4:
            u = u + lax.div(u, 2) * (1 - 2 * lax.rem(u, 2))
        return lax.rem(lax.div(z, per) + u, quarters)

    def pass_on(t):
        q = quarter(t)
        take(yrecv.at[t, pl.ds(0, YS - 1)], y_rs.at[t])
        total = yrecv[t, 0]
        for i in range(1, YS):
            total = total + yrecv[t, i]
        zpart[pl.ds(pl.multiple_of(q * 128, 128), 128), :] = total.T
        for i in range(per):
            o = q * per + i
            src = zpart.at[pl.ds(pl.multiple_of(o * piece, piece), piece), :]

            @pl.when(o != z)
            def _(o=o, src=src):
                send(src, zrecv.at[z], fz_ss, fz_rs, at(k, y, o))

            @pl.when(o == z)
            def _(o=o, src=src):
                zrecv[z] = src[...]

    def gradient_step(t, carry):
        q = quarter(t)
        grad_chunk(1 - k, q, bench_part.at[t])
        send(bench_part.at[t], sib.at[t], sib_ss, sib_rs.at[t], sibling)
        grad_chunk(k, q, ysend.at[t])
        take(sib.at[t], sib_rs.at[t])
        for o in range(YS):
            s = slice(o * 128, (o + 1) * 128)
            ysend[t, :, s] = ysend[t, :, s] + sib[t, :, s]

            @pl.when(o != y)
            def _(o=o, s=s):
                send(ysend.at[t, :, s], yrecv.at[t, y], y_ss, y_rs.at[t], at(k, o, z))

            @pl.when(o == y)
            def _(o=o, s=s):
                yrecv[t, y] = ysend[t, :, s]

        @pl.when(t >= 2)
        def _():
            pass_on(t - 2)

        return carry

    lax.fori_loop(0, quarters, gradient_step, 0)

    quarter_rows = rows // nx
    mine_rows = pl.ds(pl.multiple_of(c * quarter_rows, quarter_rows), quarter_rows)
    for p in x_peers:
        there = pl.ds(pl.multiple_of(p[1] * quarter_rows, quarter_rows), quarter_rows)
        send(crawl_acc.at[there, :], crawl_recv.at[c], cr_ss, cr_rs, p)
    crawl_recv[c] = crawl_acc[mine_rows, :]

    for t in range(max(quarters - 2, 0), quarters):
        pass_on(t)

    take(crawl_recv.at[pl.ds(0, nx - 1)], cr_rs)
    crawl_out[mine_rows, :] = summed(crawl_recv, nx)
    for p in x_peers:
        send(crawl_out.at[mine_rows, :], crawl_out.at[mine_rows, :], ca_ss, ca_rs, p)

    def place(y_, z_):
        return bench_out.at[pl.ds(pl.multiple_of(k * half + y_ * part + z_ * piece, piece), piece), :]

    def back(v, d, n):
        return lax.rem(v + n - d, n)

    take(zrecv.at[pl.ds(0, nz - 1)], fz_rs)
    place(y, z)[...] = summed(zrecv, nz)
    y_up, y_down = at(k, lax.rem(y + 1, YS), z), at(k, lax.rem(y + YS - 1, YS), z)
    z_up, z_down = at(k, y, lax.rem(z + 1, nz)), at(k, y, lax.rem(z + nz - 1, nz))
    ups = nz // 2

    def forward(d):
        got = place(y, back(z, d, nz))
        if d:
            take(got, gz_rs.at[d - 1])
        if d < ups:
            send(got, got, gz_ss, gz_rs.at[d], z_up)
        if d == 0 and nz > 2 or d > ups + 1:
            send(got, got, gz_ss, gz_rs.at[(d or nz) - 2], z_down)
        send(got, got, gy_ss, gy_rs.at[0, d], y_up)
        send(got, got, gy_ss, gy_rs.at[2, d], y_down)
        send(got, got, gc_ss, gc_rs, sibling)

    def relay(d):
        for e, p, first in ((1, y_up, 0), (3, y_down, 1)):
            y_, z_ = back(y, e, YS), back(z, d, nz)
            got = place(y_, z_)
            take(got, gy_rs.at[e - 1, d])
            start_ = k * half + y_ * part + z_ * piece + first * (piece // 2)
            some = bench_out.at[pl.ds(pl.multiple_of(start_, piece // 2), piece // 2), :]
            send(some, some, gy_ss, gy_rs.at[1, d], p)
            send(got, got, gc_ss, gc_rs, sibling)

    def last(d):
        got = place(back(y, 2, YS), back(z, d, nz))
        take(got, gy_rs.at[1, d])
        send(got, got, gc_ss, gc_rs, sibling)

    order = sorted(range(nz), key=lambda d: min(d, nz - d))
    lags = (3, 6)
    for i in range(nz + lags[1]):
        if i < nz:
            forward(order[i])
        if 0 <= i - lags[0] < nz:
            relay(order[i - lags[0]])
        if 0 <= i - lags[1] < nz:
            last(order[i - lags[1]])

    take(crawl_recv.at[pl.ds(0, nx - 1)], ca_rs)
    take(crawl_recv.at[pl.ds(0, nx - 1)], ca_ss)
    take(crawl_recv.at[pl.ds(0, nx - 1)], cr_ss)
    take(bench_out.at[pl.ds(0, half), :], gc_rs)
    take(bench_out.at[pl.ds(0, half), :], gc_ss)
    take(bench_out.at[pl.ds(0, half - part), :], gy_ss)
    take(zrecv.at[pl.ds(0, nz - 1)], gz_ss)
    take(zrecv.at[pl.ds(0, nz - 1)], fz_ss)
    take(yrecv.at[:, pl.ds(0, YS - 1)], y_ss)
    take(sib, sib_ss)


def solution(mesh):
    nx = mesh.shape["cols"]
    nz = mesh.shape["rows"] // (CORES * YS)
    na = CORES * YS

    def per_device(crawl, bench, start_duals, row_cotangent, col_cotangent):
        rows, depth = crawl.shape
        cols = bench.shape[0]
        half, part = cols // CORES, cols // (CORES * YS)
        vmem, dma = pltpu.VMEM, pltpu.SemaphoreType.DMA
        scratch = [
            vmem((rows, cols), F32),
            vmem((depth, rows), jnp.bfloat16),
            vmem((rows, 128), F32),
            vmem((rows, 128), F32),
            vmem((rows, 128), F32),
            vmem((rows, 128), F32),
            vmem((1, rows), F32),
            *[vmem((1, cols), F32)] * 5,
            vmem((2, rows), F32), vmem((nx, 2, rows), F32),
            vmem((3, 1, rows), F32), vmem((3, nx, 1, rows), F32),
            vmem((CORES, 2, half), F32), vmem((na, 2, half), F32),
            vmem((2, CORES, 1, half), F32), vmem((2, na, 1, half), F32),
            vmem((2, half), F32), vmem((nz, 2, half), F32),
            vmem((2, 1, half), F32), vmem((2, nz, 1, half), F32),
            vmem((3, CORES, 1, half), F32),
            vmem((rows, depth), F32), vmem((nx, rows // nx, depth), F32),
            vmem((part // 128, depth, YS * 128), F32), vmem((part // 128, depth, YS * 128), F32),
            vmem((part // 128, depth, YS * 128), F32), vmem((part // 128, YS, depth, 128), F32),
            vmem((part, depth), F32), vmem((nz, part // nz, depth), F32),
            dma((4,)), dma((4,)), dma((3,)), dma((3,)), dma((3,)), dma((3,)), dma((3,)), dma((3,)),
            dma, dma, dma, dma,
            dma, dma((part // 128,)), dma, dma((part // 128,)), dma, dma,
            dma, dma((nz - 1,)), dma, dma((YS - 1, nz)), dma, dma,
        ]
        return pl.pallas_call(
            functools.partial(kernel, nx, nz),
            out_shape=(jax.ShapeDtypeStruct((rows, depth), F32), jax.ShapeDtypeStruct((cols, depth), F32)),
            in_specs=[pl.BlockSpec(memory_space=vmem)] * 5,
            out_specs=(pl.BlockSpec(memory_space=vmem),) * 2,
            scratch_shapes=scratch,
            compiler_params=pltpu.CompilerParams(
                collective_id=0, has_side_effects=True, vmem_limit_bytes=56 << 20
            ),
        )(crawl, bench, start_duals[None, :], row_cotangent[None, :], col_cotangent[None, :])

    placed = (P("rows", None), P("cols", None), P("cols"), P("rows"), P("cols"))
    return jax.shard_map(
        per_device,
        mesh=mesh,
        in_specs=placed,
        out_specs=(P("rows", None), P("cols", None)),
        check_vma=False,
    )
```

```python
import functools
import math

import jax
import jax.numpy as jnp
from jax import lax
from jax.experimental import pallas as pl
from jax.experimental.pallas import tpu as pltpu
from jax.sharding import PartitionSpec as P

EPSILON = 0.05
SCALE = math.log2(math.e) / EPSILON
MESH = pl.DeviceIdType.MESH
F32 = jnp.float32
CORES, YS = 2, 4


def kernel(
    nx, nz,
    crawl_in, bench_in, start_in, row_cot_in, col_cot_in,
    crawl_out, bench_out,
    crawl, bench, start, row_cot, col_cot, in_s, tile, crawl_t, lane_max, alpha_b, beta_b, back_b,
    kept, rowvec, colmax, fvec, gvec, avec, bvec,
    xs1, xr1, xs, xr, as1, ar1, as_, ar, zs1, zr1, zs, zr, cg,
    crawl_acc, crawl_recv, bench_part, sib, ysend, yrecv, zpart, zrecv,
    x_ss, x_rs, a_ss, a_rs, z_ss, z_rs, g_ss, g_rs,
    cr_ss, cr_rs, ca_ss, ca_rs, sib_ss, sib_rs, y_ss, y_rs, fz_ss, fz_rs,
    gz_ss, gz_rs, gy_ss, gy_rs, gc_ss, gc_rs,
):
    rows, depth = crawl.shape
    cols = bench.shape[0]
    half, part = cols // CORES, cols // (CORES * YS)
    na = CORES * YS
    r, c = lax.axis_index("rows"), lax.axis_index("cols")
    k, y, z = lax.rem(r, CORES), lax.rem(lax.div(r, CORES), YS), lax.div(r, na)
    a = lax.rem(r, na)

    def at(k_, y_, z_):
        return ((z_ * YS + y_) * CORES + k_, c)

    x_peers = [(r, lax.rem(c + d, nx)) for d in range(1, nx)]
    a_peers = []
    for d in range(1, na):
        o = lax.rem(a + d, na)
        a_peers.append((lax.rem(o, CORES), at(lax.rem(o, CORES), lax.div(o, CORES), z)))
    z_peers = [(lax.rem(z + d, nz), at(k, y, lax.rem(z + d, nz))) for d in range(1, nz)]
    sibling = at(1 - k, y, z)

    loads = [
        pltpu.make_async_copy(src, dst, in_s.at[i])
        for i, (src, dst) in enumerate((
            (crawl_in, crawl), (bench_in, bench), (start_in, start), (row_cot_in, row_cot), (col_cot_in, col_cot),
        ))
    ]
    for load in loads:
        load.start()

    barrier = pltpu.get_barrier_semaphore()
    everyone = x_peers + [p for _, p in a_peers] + [p for _, p in z_peers]
    for p in everyone:
        pl.semaphore_signal(barrier, inc=1, device_id=p, device_id_type=MESH)

    def send(src, dst, ss, rs, p):
        pltpu.make_async_remote_copy(
            src_ref=src, dst_ref=dst, send_sem=ss, recv_sem=rs, device_id=p, device_id_type=MESH
        ).start()

    def take(ref, sem):
        pltpu.make_async_copy(ref, ref, sem).wait()

    hr = rows // 2
    halves = [slice(h * hr, (h + 1) * hr) for h in range(2)]

    def x_send(n, h, src, recv):
        s = halves[h]
        recv[c, :, s] = src[:, s]
        for p in x_peers:
            send(src.at[:, s], recv.at[c, :, s], x_ss.at[n, h], x_rs.at[n, h], p)

    def x_take(n, h, recv):
        others = recv.at[pl.ds(0, nx - 1), :, halves[h]]
        take(others, x_rs.at[n, h])
        take(others, x_ss.at[n, h])

    def a_exchange(n, src, recv):
        recv[a] = src[k]
        for o, p in a_peers:
            send(src.at[o], recv.at[a], a_ss.at[n], a_rs.at[n], p)
        others = recv.at[pl.ds(0, na - 1)]
        take(others, a_rs.at[n])
        take(others, a_ss.at[n])

    def z_exchange(n, src, recv):
        recv[z] = src[...]
        for _, p in z_peers:
            send(src, recv.at[z], z_ss.at[n], z_rs.at[n], p)
        others = recv.at[pl.ds(0, nz - 1)]
        take(others, z_rs.at[n])
        take(others, z_ss.at[n])

    def core_gather(n, value):
        cg[n, k] = value
        send(cg.at[n, k], cg.at[n, k], g_ss.at[n], g_rs.at[n], sibling)
        take(cg.at[n, k], g_rs.at[n])
        take(cg.at[n, k], g_ss.at[n])

    def summed(recv, n, s=slice(None)):
        total = recv[0, :, s]
        for i in range(1, n):
            total = total + recv[i, :, s]
        return total

    def combined(recv, n, s=slice(None)):
        top = recv[0, 0:1, s]
        for i in range(1, n):
            top = jnp.maximum(top, recv[i, 0:1, s])
        total = recv[0, 1:2, s] * jnp.exp2(recv[0, 0:1, s] - top)
        for i in range(1, n):
            total = total + recv[i, 1:2, s] * jnp.exp2(recv[i, 0:1, s] - top)
        return top, total

    def spread(vec, out, h):
        for i in range(hr // 128):
            piece = vec[:, i * 128 : (i + 1) * 128]
            o = h * hr + i * 128
            out[o : o + 128, :] = jnp.broadcast_to(piece, (128, 128)).T

    def row_pass(d, n):
        out = xs.at[n]

        def step(i, carry):
            base = pl.multiple_of(i * 128, 128)
            pieces = []
            for h in range(2):
                acc = jnp.zeros((64, 128), F32)
                for j in range(cols // 128):
                    s = slice(j * 128, (j + 1) * 128)
                    acc = acc + tile[pl.ds(base + h * 64, 64), s] * d[0:1, s]
                pieces.append(acc)
            acc = jnp.concatenate(pieces, 0).T
            out[0:1, pl.ds(base, 128)] = jnp.sum(acc, 0, keepdims=True)
            return carry

        for h in range(2):
            lax.fori_loop(h * (hr // 128), (h + 1) * (hr // 128), step, 0)
            x_send(n + 1, h, out, xr.at[n])

    width = min(1024, cols)

    def col_loop(h, init, step, keep, finish):
        for cb in range(cols // width):
            at_ = [slice(cb * width + j * 128, cb * width + (j + 1) * 128) for j in range(width // 128)]
            first = tuple(jnp.full((8, 128), init, F32) if h == 0 else keep[:, s] for s in at_)
            last_ = lax.fori_loop(
                h * (hr // 64), (h + 1) * (hr // 64), lambda i, accs, at_=at_: step(i, accs, at_), first
            )
            for s, acc in zip(at_, last_):
                if h == 0:
                    keep[:, s] = acc
                else:
                    finish(s, acc)

    def col_pass(w, ready, finish):
        def step(i, accs, at_):
            base = pl.multiple_of(i * 64, 64)
            wb = w[pl.ds(base, 64), :]
            return tuple(
                acc + jnp.sum((tile[pl.ds(base, 64), s] * wb).reshape(8, 8, 128), 0) for acc, s in zip(accs, at_)
            )

        for h in range(2):
            ready(h)
            col_loop(h, 0.0, step, kept, lambda s, acc: finish(s.start, jnp.sum(acc, 0, keepdims=True)))

    for load in loads:
        load.wait()
    crawl_t[...] = crawl[...].astype(F32).T.astype(jnp.bfloat16)
    lane_max[...] = jnp.full(lane_max.shape, -jnp.inf, F32)
    mm = min(512, cols)
    rb = min(256, rows)

    def score_step(t, carry):
        i, jb = lax.rem(t, rows // rb), lax.div(t, rows // rb)
        base = pl.multiple_of(i * rb, rb)
        off = pl.multiple_of(jb * mm, mm)
        s = lax.dot_general(
            crawl[pl.ds(base, rb), :], bench[pl.ds(off, mm), :], (((1,), (1,)), ((), ())),
            preferred_element_type=F32,
        )
        s = s * SCALE + start[0:1, pl.ds(off, mm)] * SCALE
        tile[pl.ds(base, rb), pl.ds(off, mm)] = s
        top = lane_max[pl.ds(base, rb), :]
        for j in range(mm // 128):
            top = jnp.maximum(top, s[:, j * 128 : (j + 1) * 128])
        lane_max[pl.ds(base, rb), :] = top
        return carry

    lax.fori_loop(0, (rows // rb) * (cols // mm), score_step, 0, unroll=4)

    def level_step(i, carry):
        base = pl.multiple_of(i * 128, 128)
        tops, sums = [], []
        for h in range(2):
            at_ = pl.ds(base + h * 64, 64)
            top = lane_max[at_, :]
            acc = jnp.zeros((64, 128), F32)
            for j in range(cols // 128):
                acc = acc + jnp.exp2(tile[at_, j * 128 : (j + 1) * 128] - top)
            tops.append(top)
            sums.append(acc)
        top = jnp.concatenate(tops, 0).T
        acc = jnp.concatenate(sums, 0).T
        best = jnp.max(top, 0, keepdims=True)
        xs1[0:1, pl.ds(base, 128)] = best
        xs1[1:2, pl.ds(base, 128)] = jnp.sum(acc * jnp.exp2(top - best), 0, keepdims=True)
        return carry

    for h in range(2):
        lax.fori_loop(h * (hr // 128), (h + 1) * (hr // 128), level_step, 0)
        if h == 0:
            pl.semaphore_wait(barrier, len(everyone))
        x_send(0, h, xs1, xr1)

    def top_step(i, tops, at_):
        base = pl.multiple_of(i * 64, 64)
        lev = alpha_b[pl.ds(base, 64), :]
        return tuple(
            jnp.maximum(top, jnp.max((tile[pl.ds(base, 64), s] - lev).reshape(8, 8, 128), 0))
            for top, s in zip(tops, at_)
        )

    def top_finish(s, top):
        colmax[0:1, s] = jnp.max(top, 0, keepdims=True)

    for h in range(2):
        x_take(0, h, xr1)
        top, total = combined(xr1, nx, halves[h])
        spread(top + jnp.log2(total), alpha_b, h)
        col_loop(h, -jnp.inf, top_step, kept, top_finish)

    for cb in range(cols // width):
        def exp_step(i, accs, cb=cb):
            base = pl.multiple_of(i * 64, 64)
            lev = alpha_b[pl.ds(base, 64), :]
            new = []
            for j in range(width // 128):
                o = cb * width + j * 128
                e = jnp.exp2((tile[pl.ds(base, 64), o : o + 128] - lev) - colmax[0:1, o : o + 128])
                tile[pl.ds(base, 64), o : o + 128] = e
                new.append(accs[j] + jnp.sum(e.reshape(8, 8, 128), 0))
            return tuple(new)

        accs = lax.fori_loop(
            0, rows // 64, exp_step, tuple(jnp.zeros((8, 128), F32) for _ in range(width // 128))
        )
        for j in range(width // 128):
            o = cb * width + j * 128
            h, p = o // half, o % half
            as1[h, 0:1, p : p + 128] = colmax[0:1, o : o + 128]
            as1[h, 1:2, p : p + 128] = jnp.sum(accs[j], 0, keepdims=True)
    gvec[...] = jnp.exp2(colmax[...])

    a_exchange(0, as1, ar1)
    top, total = combined(ar1, na)
    zs1[0:1, :] = top
    zs1[1:2, :] = total
    z_exchange(0, zs1, zr1)
    top, total = combined(zr1, nz)
    core_gather(0, top + jnp.log2(total))
    for h in range(CORES):
        s = slice(h * half, (h + 1) * half)
        fvec[0:1, s] = jnp.exp2(colmax[0:1, s] - cg[0, h])

    row_pass(fvec, 0)

    def alpha_ready(h):
        x_take(1, h, xr.at[0])
        alpha = 1.0 / summed(xr.at[0], nx, halves[h])
        rowvec[:, halves[h]] = alpha
        spread(alpha, alpha_b, h)

    def col_reduce(n, w, ready):
        def finish(o, v):
            h, p = o // half, o % half
            as_[n, h, 0:1, p : p + 128] = v * fvec[0:1, o : o + 128]

        col_pass(w, ready, finish)
        a_exchange(n + 1, as_.at[n], ar.at[n])
        zs[n] = summed(ar.at[n], na)
        z_exchange(n + 1, zs.at[n], zr.at[n])
        core_gather(n + 1, summed(zr.at[n], nz))

    col_reduce(0, alpha_b, alpha_ready)
    for h in range(CORES):
        s = slice(h * half, (h + 1) * half)
        avec[0:1, s] = fvec[0:1, s] * col_cot[0:1, s] / cg[1, h]

    row_pass(avec, 1)

    def beta_ready(h):
        x_take(2, h, xr.at[1])
        alpha = rowvec[:, halves[h]]
        back2 = row_cot[:, halves[h]] - alpha * summed(xr.at[1], nx, halves[h])
        spread(back2 * alpha, beta_b, h)

    col_reduce(1, beta_b, beta_ready)
    for h in range(CORES):
        s = slice(h * half, (h + 1) * half)
        bvec[0:1, s] = -fvec[0:1, s] * cg[2, h]

    row_pass(bvec, 2)
    for h in range(2):
        x_take(3, h, xr.at[2])
        spread(-summed(xr.at[2], nx, halves[h]), back_b, h)

    crawl_acc[...] = jnp.zeros(crawl_acc.shape, F32)

    def grad_chunk(core, q, out):
        offs = [pl.multiple_of(core * half + o * part + q * 128, 128) for o in range(YS)]
        some_bench = jnp.concatenate([bench[pl.ds(o, 128), :] for o in offs], 0)
        acc = None
        for i in range(rows // rb):
            blocks = []
            for h in range(rb // 64):
                at_ = slice(i * rb + h * 64, i * rb + (h + 1) * 64)
                al, be, ba = alpha_b[at_, :], beta_b[at_, :], back_b[at_, :]
                pieces = []
                for o in offs:
                    s = pl.ds(o, 128)
                    bracket = (al * avec[0:1, s] + be * fvec[0:1, s]) + (bvec[0:1, s] + ba * gvec[0:1, s])
                    pieces.append((-(tile[at_, s] * bracket)).astype(jnp.bfloat16))
                blocks.append(jnp.concatenate(pieces, 1))
            grads = jnp.concatenate(blocks, 0)
            at_ = slice(i * rb, (i + 1) * rb)
            crawl_acc[at_, :] += jnp.dot(grads, some_bench, preferred_element_type=F32)
            product = jnp.dot(crawl_t[:, at_], grads, preferred_element_type=F32)
            acc = product if acc is None else acc + product
        out[...] = acc

    piece = part // nz
    quarters = part // 128
    per = nz // quarters

    def quarter(t):
        u = quarters - 1 - t
        if quarters == 4:
            u = u + lax.div(u, 2) * (1 - 2 * lax.rem(u, 2))
        return lax.rem(lax.div(z, per) + u, quarters)

    def pass_on(t):
        q = quarter(t)
        take(yrecv.at[t, pl.ds(0, YS - 1)], y_rs.at[t])
        total = yrecv[t, 0]
        for i in range(1, YS):
            total = total + yrecv[t, i]
        zpart[pl.ds(pl.multiple_of(q * 128, 128), 128), :] = total.T
        for i in range(per):
            o = q * per + i
            src = zpart.at[pl.ds(pl.multiple_of(o * piece, piece), piece), :]

            @pl.when(o != z)
            def _(o=o, src=src):
                send(src, zrecv.at[z], fz_ss, fz_rs, at(k, y, o))

            @pl.when(o == z)
            def _(o=o, src=src):
                zrecv[z] = src[...]

    def gradient_step(t, carry):
        q = quarter(t)
        grad_chunk(1 - k, q, bench_part.at[t])
        send(bench_part.at[t], sib.at[t], sib_ss, sib_rs.at[t], sibling)
        grad_chunk(k, q, ysend.at[t])
        take(sib.at[t], sib_rs.at[t])
        for o in range(YS):
            s = slice(o * 128, (o + 1) * 128)
            ysend[t, :, s] = ysend[t, :, s] + sib[t, :, s]

            @pl.when(o != y)
            def _(o=o, s=s):
                send(ysend.at[t, :, s], yrecv.at[t, y], y_ss, y_rs.at[t], at(k, o, z))

            @pl.when(o == y)
            def _(o=o, s=s):
                yrecv[t, y] = ysend[t, :, s]

        @pl.when(t >= 2)
        def _():
            pass_on(t - 2)

        return carry

    lax.fori_loop(0, quarters, gradient_step, 0)

    quarter_rows = rows // nx
    mine_rows = pl.ds(pl.multiple_of(c * quarter_rows, quarter_rows), quarter_rows)
    for p in x_peers:
        there = pl.ds(pl.multiple_of(p[1] * quarter_rows, quarter_rows), quarter_rows)
        send(crawl_acc.at[there, :], crawl_recv.at[c], cr_ss, cr_rs, p)
    crawl_recv[c] = crawl_acc[mine_rows, :]

    for t in range(max(quarters - 2, 0), quarters):
        pass_on(t)

    take(crawl_recv.at[pl.ds(0, nx - 1)], cr_rs)
    crawl_out[mine_rows, :] = summed(crawl_recv, nx)
    for p in x_peers:
        send(crawl_out.at[mine_rows, :], crawl_out.at[mine_rows, :], ca_ss, ca_rs, p)

    def place(y_, z_):
        return bench_out.at[pl.ds(pl.multiple_of(k * half + y_ * part + z_ * piece, piece), piece), :]

    def back(v, d, n):
        return lax.rem(v + n - d, n)

    take(zrecv.at[pl.ds(0, nz - 1)], fz_rs)
    place(y, z)[...] = summed(zrecv, nz)
    y_up, y_down = at(k, lax.rem(y + 1, YS), z), at(k, lax.rem(y + YS - 1, YS), z)
    z_up, z_down = at(k, y, lax.rem(z + 1, nz)), at(k, y, lax.rem(z + nz - 1, nz))
    ups = nz // 2

    def forward(d):
        got = place(y, back(z, d, nz))
        if d:
            take(got, gz_rs.at[d - 1])
        if d < ups:
            send(got, got, gz_ss, gz_rs.at[d], z_up)
        if d == 0 and nz > 2 or d > ups + 1:
            send(got, got, gz_ss, gz_rs.at[(d or nz) - 2], z_down)
        send(got, got, gy_ss, gy_rs.at[0, d], y_up)
        send(got, got, gy_ss, gy_rs.at[2, d], y_down)
        send(got, got, gc_ss, gc_rs, sibling)

    def relay(d):
        for e, p, first in ((1, y_up, 0), (3, y_down, 1)):
            y_, z_ = back(y, e, YS), back(z, d, nz)
            got = place(y_, z_)
            take(got, gy_rs.at[e - 1, d])
            start_ = k * half + y_ * part + z_ * piece + first * (piece // 2)
            some = bench_out.at[pl.ds(pl.multiple_of(start_, piece // 2), piece // 2), :]
            send(some, some, gy_ss, gy_rs.at[1, d], p)
            send(got, got, gc_ss, gc_rs, sibling)

    def last(d):
        got = place(back(y, 2, YS), back(z, d, nz))
        take(got, gy_rs.at[1, d])
        send(got, got, gc_ss, gc_rs, sibling)

    order = sorted(range(nz), key=lambda d: min(d, nz - d))
    lags = (3, 6)
    for i in range(nz + lags[1]):
        if i < nz:
            forward(order[i])
        if 0 <= i - lags[0] < nz:
            relay(order[i - lags[0]])
        if 0 <= i - lags[1] < nz:
            last(order[i - lags[1]])

    take(crawl_recv.at[pl.ds(0, nx - 1)], ca_rs)
    take(crawl_recv.at[pl.ds(0, nx - 1)], ca_ss)
    take(crawl_recv.at[pl.ds(0, nx - 1)], cr_ss)
    take(bench_out.at[pl.ds(0, half), :], gc_rs)
    take(bench_out.at[pl.ds(0, half), :], gc_ss)
    take(bench_out.at[pl.ds(0, half - part), :], gy_ss)
    take(zrecv.at[pl.ds(0, nz - 1)], gz_ss)
    take(zrecv.at[pl.ds(0, nz - 1)], fz_ss)
    take(yrecv.at[:, pl.ds(0, YS - 1)], y_ss)
    take(sib, sib_ss)


def solution(mesh):
    nx = mesh.shape["cols"]
    nz = mesh.shape["rows"] // (CORES * YS)
    na = CORES * YS

    def per_device(crawl, bench, start_duals, row_cotangent, col_cotangent):
        rows, depth = crawl.shape
        cols = bench.shape[0]
        half, part = cols // CORES, cols // (CORES * YS)
        vmem, dma = pltpu.VMEM, pltpu.SemaphoreType.DMA
        scratch = [
            vmem((rows, depth), jnp.bfloat16), vmem((cols, depth), jnp.bfloat16),
            vmem((1, cols), F32), vmem((1, rows), F32), vmem((1, cols), F32), dma((5,)),
            vmem((rows, cols), F32),
            vmem((depth, rows), jnp.bfloat16),
            vmem((rows, 128), F32),
            vmem((rows, 128), F32),
            vmem((rows, 128), F32),
            vmem((rows, 128), F32),
            vmem((8, cols), F32), vmem((1, rows), F32),
            *[vmem((1, cols), F32)] * 5,
            vmem((2, rows), F32), vmem((nx, 2, rows), F32),
            vmem((3, 1, rows), F32), vmem((3, nx, 1, rows), F32),
            vmem((CORES, 2, half), F32), vmem((na, 2, half), F32),
            vmem((2, CORES, 1, half), F32), vmem((2, na, 1, half), F32),
            vmem((2, half), F32), vmem((nz, 2, half), F32),
            vmem((2, 1, half), F32), vmem((2, nz, 1, half), F32),
            vmem((3, CORES, 1, half), F32),
            vmem((rows, depth), F32), vmem((nx, rows // nx, depth), F32),
            vmem((part // 128, depth, YS * 128), F32), vmem((part // 128, depth, YS * 128), F32),
            vmem((part // 128, depth, YS * 128), F32), vmem((part // 128, YS, depth, 128), F32),
            vmem((part, depth), F32), vmem((nz, part // nz, depth), F32),
            dma((4, 2)), dma((4, 2)), dma((3,)), dma((3,)), dma((3,)), dma((3,)), dma((3,)), dma((3,)),
            dma, dma, dma, dma,
            dma, dma((part // 128,)), dma, dma((part // 128,)), dma, dma,
            dma, dma((nz - 1,)), dma, dma((YS - 1, nz)), dma, dma,
        ]
        return pl.pallas_call(
            functools.partial(kernel, nx, nz),
            out_shape=(vmem((rows, depth), F32), vmem((cols, depth), F32)),
            in_specs=[pl.BlockSpec(memory_space=pltpu.HBM)] * 5,
            out_specs=(pl.BlockSpec(memory_space=vmem),) * 2,
            scratch_shapes=scratch,
            compiler_params=pltpu.CompilerParams(
                collective_id=0, has_side_effects=True, vmem_limit_bytes=56 << 20
            ),
        )(crawl, bench, start_duals[None, :], row_cotangent[None, :], col_cotangent[None, :])

    placed = (P("rows", None), P("cols", None), P("cols"), P("rows"), P("cols"))
    return jax.shard_map(
        per_device,
        mesh=mesh,
        in_specs=placed,
        out_specs=(P("rows", None), P("cols", None)),
        check_vma=False,
    )
```

```python
import functools
import math

import jax
import jax.numpy as jnp
from jax import lax
from jax.experimental import pallas as pl
from jax.experimental.pallas import tpu as pltpu
from jax.sharding import PartitionSpec as P

EPSILON = 0.05
SCALE = math.log2(math.e) / EPSILON
MESH = pl.DeviceIdType.MESH
F32 = jnp.float32
CORES, YS = 2, 4


def kernel(
    nx, nz,
    crawl_in, bench_in, start_in, row_cot_in, col_cot_in,
    crawl_out, bench_out,
    crawl, bench, start, row_cot, col_cot, in_s, tile, crawl_t, lane_max, alpha_b, beta_b, back_b,
    kept, rowvec, colmax, fvec, gvec, avec, bvec,
    xs1, xr1, xs, xr, as1, ar1, as_, ar, zs1, zr1, zs, zr, cg,
    crawl_acc, crawl_recv, bench_part, sib, ysend, yrecv, zpart, zrecv,
    x_ss, x_rs, a_ss, a_rs, z_ss, z_rs, g_ss, g_rs,
    cr_ss, cr_rs, ca_ss, ca_rs, sib_ss, sib_rs, y_ss, y_rs, fz_ss, fz_rs,
    gz_ss, gz_rs, gy_ss, gy_rs, gc_ss, gc_rs,
):
    rows, depth = crawl.shape
    cols = bench.shape[0]
    half, part = cols // CORES, cols // (CORES * YS)
    na = CORES * YS
    r, c = lax.axis_index("rows"), lax.axis_index("cols")
    k, y, z = lax.rem(r, CORES), lax.rem(lax.div(r, CORES), YS), lax.div(r, na)
    a = lax.rem(r, na)

    def at(k_, y_, z_):
        return ((z_ * YS + y_) * CORES + k_, c)

    x_peers = [(r, lax.rem(c + d, nx)) for d in sorted(range(1, nx), key=lambda d: -min(d, nx - d))]
    a_peers = []
    for d in (4, 5, 3, 2, 6, 7, 1):
        o = lax.rem(a + d, na)
        a_peers.append((lax.rem(o, CORES), at(lax.rem(o, CORES), lax.div(o, CORES), z)))
    by_far = sorted(range(1, nz), key=lambda d: -min(d, nz - d))
    z_peers = [(lax.rem(z + d, nz), at(k, y, lax.rem(z + d, nz))) for d in by_far]
    sibling = at(1 - k, y, z)

    loads = [
        pltpu.make_async_copy(src, dst, in_s.at[i])
        for i, (src, dst) in enumerate((
            (crawl_in, crawl), (bench_in, bench), (start_in, start), (row_cot_in, row_cot), (col_cot_in, col_cot),
        ))
    ]
    for load in loads:
        load.start()

    barrier = pltpu.get_barrier_semaphore()
    everyone = x_peers + [p for _, p in a_peers] + [p for _, p in z_peers]
    for p in everyone:
        pl.semaphore_signal(barrier, inc=1, device_id=p, device_id_type=MESH)

    def send(src, dst, ss, rs, p):
        pltpu.make_async_remote_copy(
            src_ref=src, dst_ref=dst, send_sem=ss, recv_sem=rs, device_id=p, device_id_type=MESH
        ).start()

    def take(ref, sem):
        pltpu.make_async_copy(ref, ref, sem).wait()

    hr = rows // 2
    halves = [slice(h * hr, (h + 1) * hr) for h in range(2)]

    def x_send(n, h, src, recv):
        s = halves[h]
        recv[c, :, s] = src[:, s]
        for p in x_peers:
            send(src.at[:, s], recv.at[c, :, s], x_ss.at[n, h], x_rs.at[n, h], p)

    def x_take(n, h, recv):
        others = recv.at[pl.ds(0, nx - 1), :, halves[h]]
        take(others, x_rs.at[n, h])
        take(others, x_ss.at[n, h])

    def a_exchange(n, src, recv):
        recv[a] = src[k]
        for o, p in a_peers:
            send(src.at[o], recv.at[a], a_ss.at[n], a_rs.at[n], p)
        others = recv.at[pl.ds(0, na - 1)]
        take(others, a_rs.at[n])
        take(others, a_ss.at[n])

    def z_exchange(n, src, recv):
        recv[z] = src[...]
        for _, p in z_peers:
            send(src, recv.at[z], z_ss.at[n], z_rs.at[n], p)
        others = recv.at[pl.ds(0, nz - 1)]
        take(others, z_rs.at[n])
        take(others, z_ss.at[n])

    def core_gather(n, value):
        cg[n, k] = value
        send(cg.at[n, k], cg.at[n, k], g_ss.at[n], g_rs.at[n], sibling)
        take(cg.at[n, k], g_rs.at[n])
        take(cg.at[n, k], g_ss.at[n])

    def summed(recv, n, s=slice(None)):
        total = recv[0, :, s]
        for i in range(1, n):
            total = total + recv[i, :, s]
        return total

    def combined(recv, n, s=slice(None)):
        top = recv[0, 0:1, s]
        for i in range(1, n):
            top = jnp.maximum(top, recv[i, 0:1, s])
        total = recv[0, 1:2, s] * jnp.exp2(recv[0, 0:1, s] - top)
        for i in range(1, n):
            total = total + recv[i, 1:2, s] * jnp.exp2(recv[i, 0:1, s] - top)
        return top, total

    def spread(vec, out, h):
        for i in range(hr // 128):
            piece = vec[:, i * 128 : (i + 1) * 128]
            o = h * hr + i * 128
            out[o : o + 128, :] = jnp.broadcast_to(piece, (128, 128)).T

    def row_pass(d, n):
        out = xs.at[n]

        def step(i, carry):
            base = pl.multiple_of(i * 128, 128)
            pieces = []
            for h in range(2):
                acc = jnp.zeros((64, 128), F32)
                for j in range(cols // 128):
                    s = slice(j * 128, (j + 1) * 128)
                    acc = acc + tile[pl.ds(base + h * 64, 64), s] * d[0:1, s]
                pieces.append(acc)
            acc = jnp.concatenate(pieces, 0).T
            out[0:1, pl.ds(base, 128)] = jnp.sum(acc, 0, keepdims=True)
            return carry

        for h in range(2):
            lax.fori_loop(h * (hr // 128), (h + 1) * (hr // 128), step, 0, unroll=2)
            x_send(n + 1, h, out, xr.at[n])

    width = min(1024, cols)

    def col_loop(h, init, step, keep, finish):
        for cb in range(cols // width):
            at_ = [slice(cb * width + j * 128, cb * width + (j + 1) * 128) for j in range(width // 128)]
            first = tuple(jnp.full((8, 128), init, F32) if h == 0 else keep[:, s] for s in at_)
            last_ = lax.fori_loop(
                h * (hr // 64), (h + 1) * (hr // 64), lambda i, accs, at_=at_: step(i, accs, at_), first, unroll=2
            )
            for s, acc in zip(at_, last_):
                if h == 0:
                    keep[:, s] = acc
                else:
                    finish(s, acc)

    def col_pass(w, ready, finish):
        def step(i, accs, at_):
            base = pl.multiple_of(i * 64, 64)
            wb = w[pl.ds(base, 64), :]
            return tuple(
                acc + jnp.sum((tile[pl.ds(base, 64), s] * wb).reshape(8, 8, 128), 0) for acc, s in zip(accs, at_)
            )

        for h in range(2):
            ready(h)
            col_loop(h, 0.0, step, kept, lambda s, acc: finish(s.start, jnp.sum(acc, 0, keepdims=True)))

    for load in loads:
        load.wait()
    crawl_t[...] = crawl[...].astype(F32).T.astype(jnp.bfloat16)
    lane_max[...] = jnp.full(lane_max.shape, -jnp.inf, F32)
    mm = min(512, cols)
    rb = min(256, rows)

    def score_step(t, carry):
        i, jb = lax.rem(t, rows // rb), lax.div(t, rows // rb)
        base = pl.multiple_of(i * rb, rb)
        off = pl.multiple_of(jb * mm, mm)
        s = lax.dot_general(
            crawl[pl.ds(base, rb), :], bench[pl.ds(off, mm), :], (((1,), (1,)), ((), ())),
            preferred_element_type=F32,
        )
        s = s * SCALE + start[0:1, pl.ds(off, mm)] * SCALE
        tile[pl.ds(base, rb), pl.ds(off, mm)] = s
        top = lane_max[pl.ds(base, rb), :]
        for j in range(mm // 128):
            top = jnp.maximum(top, s[:, j * 128 : (j + 1) * 128])
        lane_max[pl.ds(base, rb), :] = top
        return carry

    lax.fori_loop(0, (rows // rb) * (cols // mm), score_step, 0, unroll=8)

    def level_step(i, carry):
        base = pl.multiple_of(i * 128, 128)
        tops, sums = [], []
        for h in range(2):
            at_ = pl.ds(base + h * 64, 64)
            top = lane_max[at_, :]
            acc = jnp.zeros((64, 128), F32)
            for j in range(cols // 128):
                acc = acc + jnp.exp2(tile[at_, j * 128 : (j + 1) * 128] - top)
            tops.append(top)
            sums.append(acc)
        top = jnp.concatenate(tops, 0).T
        acc = jnp.concatenate(sums, 0).T
        best = jnp.max(top, 0, keepdims=True)
        xs1[0:1, pl.ds(base, 128)] = best
        xs1[1:2, pl.ds(base, 128)] = jnp.sum(acc * jnp.exp2(top - best), 0, keepdims=True)
        return carry

    for h in range(2):
        lax.fori_loop(h * (hr // 128), (h + 1) * (hr // 128), level_step, 0)
        if h == 0:
            pl.semaphore_wait(barrier, len(everyone))
        x_send(0, h, xs1, xr1)

    def top_step(i, tops, at_):
        base = pl.multiple_of(i * 64, 64)
        lev = alpha_b[pl.ds(base, 64), :]
        return tuple(
            jnp.maximum(top, jnp.max((tile[pl.ds(base, 64), s] - lev).reshape(8, 8, 128), 0))
            for top, s in zip(tops, at_)
        )

    def top_finish(s, top):
        colmax[0:1, s] = jnp.max(top, 0, keepdims=True)

    for h in range(2):
        x_take(0, h, xr1)
        top, total = combined(xr1, nx, halves[h])
        spread(top + jnp.log2(total), alpha_b, h)
        col_loop(h, -jnp.inf, top_step, kept, top_finish)

    for cb in range(cols // width):
        def exp_step(i, accs, cb=cb):
            base = pl.multiple_of(i * 64, 64)
            lev = alpha_b[pl.ds(base, 64), :]
            new = []
            for j in range(width // 128):
                o = cb * width + j * 128
                e = jnp.exp2((tile[pl.ds(base, 64), o : o + 128] - lev) - colmax[0:1, o : o + 128])
                tile[pl.ds(base, 64), o : o + 128] = e
                new.append(accs[j] + jnp.sum(e.reshape(8, 8, 128), 0))
            return tuple(new)

        accs = lax.fori_loop(
            0, rows // 64, exp_step, tuple(jnp.zeros((8, 128), F32) for _ in range(width // 128))
        )
        for j in range(width // 128):
            o = cb * width + j * 128
            h, p = o // half, o % half
            as1[h, 0:1, p : p + 128] = colmax[0:1, o : o + 128]
            as1[h, 1:2, p : p + 128] = jnp.sum(accs[j], 0, keepdims=True)
    gvec[...] = jnp.exp2(colmax[...])

    a_exchange(0, as1, ar1)
    top, total = combined(ar1, na)
    zs1[0:1, :] = top
    zs1[1:2, :] = total
    z_exchange(0, zs1, zr1)
    top, total = combined(zr1, nz)
    core_gather(0, top + jnp.log2(total))
    for h in range(CORES):
        s = slice(h * half, (h + 1) * half)
        fvec[0:1, s] = jnp.exp2(colmax[0:1, s] - cg[0, h])

    row_pass(fvec, 0)

    def alpha_ready(h):
        x_take(1, h, xr.at[0])
        alpha = 1.0 / summed(xr.at[0], nx, halves[h])
        rowvec[:, halves[h]] = alpha
        spread(alpha, alpha_b, h)

    def col_reduce(n, w, ready):
        def finish(o, v):
            h, p = o // half, o % half
            as_[n, h, 0:1, p : p + 128] = v * fvec[0:1, o : o + 128]

        col_pass(w, ready, finish)
        a_exchange(n + 1, as_.at[n], ar.at[n])
        zs[n] = summed(ar.at[n], na)
        z_exchange(n + 1, zs.at[n], zr.at[n])
        core_gather(n + 1, summed(zr.at[n], nz))

    col_reduce(0, alpha_b, alpha_ready)
    for h in range(CORES):
        s = slice(h * half, (h + 1) * half)
        avec[0:1, s] = fvec[0:1, s] * col_cot[0:1, s] / cg[1, h]

    row_pass(avec, 1)

    def beta_ready(h):
        x_take(2, h, xr.at[1])
        alpha = rowvec[:, halves[h]]
        back2 = row_cot[:, halves[h]] - alpha * summed(xr.at[1], nx, halves[h])
        spread(back2 * alpha, beta_b, h)

    col_reduce(1, beta_b, beta_ready)
    for h in range(CORES):
        s = slice(h * half, (h + 1) * half)
        bvec[0:1, s] = -fvec[0:1, s] * cg[2, h]

    row_pass(bvec, 2)
    for h in range(2):
        x_take(3, h, xr.at[2])
        spread(-summed(xr.at[2], nx, halves[h]), back_b, h)

    crawl_acc[...] = jnp.zeros(crawl_acc.shape, F32)

    def grad_chunk(core, q, out):
        offs = [pl.multiple_of(core * half + o * part + q * 128, 128) for o in range(YS)]
        some_bench = jnp.concatenate([bench[pl.ds(o, 128), :] for o in offs], 0)
        acc = None
        for i in range(rows // rb):
            blocks = []
            for h in range(rb // 64):
                at_ = slice(i * rb + h * 64, i * rb + (h + 1) * 64)
                al, be, ba = alpha_b[at_, :], beta_b[at_, :], back_b[at_, :]
                pieces = []
                for o in offs:
                    s = pl.ds(o, 128)
                    bracket = (al * avec[0:1, s] + be * fvec[0:1, s]) + (bvec[0:1, s] + ba * gvec[0:1, s])
                    pieces.append((-(tile[at_, s] * bracket)).astype(jnp.bfloat16))
                blocks.append(jnp.concatenate(pieces, 1))
            grads = jnp.concatenate(blocks, 0)
            at_ = slice(i * rb, (i + 1) * rb)
            crawl_acc[at_, :] += jnp.dot(grads, some_bench, preferred_element_type=F32)
            product = jnp.dot(crawl_t[:, at_], grads, preferred_element_type=F32)
            acc = product if acc is None else acc + product
        out[...] = acc

    piece = part // nz
    quarters = part // 128
    per = nz // quarters

    def quarter(t):
        u = quarters - 1 - t
        if quarters == 4:
            u = u + lax.div(u, 2) * (1 - 2 * lax.rem(u, 2))
        return lax.rem(lax.div(z, per) + u, quarters)

    def pass_on(t):
        q = quarter(t)
        take(yrecv.at[t, pl.ds(0, YS - 1)], y_rs.at[t])
        total = yrecv[t, 0]
        for i in range(1, YS):
            total = total + yrecv[t, i]
        zpart[pl.ds(pl.multiple_of(q * 128, 128), 128), :] = total.T
        for i in range(per):
            o = q * per + i
            src = zpart.at[pl.ds(pl.multiple_of(o * piece, piece), piece), :]

            @pl.when(o != z)
            def _(o=o, src=src):
                send(src, zrecv.at[z], fz_ss, fz_rs, at(k, y, o))

            @pl.when(o == z)
            def _(o=o, src=src):
                zrecv[z] = src[...]

    def gradient_step(t, carry):
        q = quarter(t)
        grad_chunk(1 - k, q, bench_part.at[t])
        send(bench_part.at[t], sib.at[t], sib_ss, sib_rs.at[t], sibling)
        grad_chunk(k, q, ysend.at[t])
        take(sib.at[t], sib_rs.at[t])
        for o in range(YS):
            s = slice(o * 128, (o + 1) * 128)
            ysend[t, :, s] = ysend[t, :, s] + sib[t, :, s]

            @pl.when(o != y)
            def _(o=o, s=s):
                send(ysend.at[t, :, s], yrecv.at[t, y], y_ss, y_rs.at[t], at(k, o, z))

            @pl.when(o == y)
            def _(o=o, s=s):
                yrecv[t, y] = ysend[t, :, s]

        @pl.when(t >= 2)
        def _():
            pass_on(t - 2)

        return carry

    lax.fori_loop(0, quarters, gradient_step, 0)

    quarter_rows = rows // nx
    mine_rows = pl.ds(pl.multiple_of(c * quarter_rows, quarter_rows), quarter_rows)
    for p in x_peers:
        there = pl.ds(pl.multiple_of(p[1] * quarter_rows, quarter_rows), quarter_rows)
        send(crawl_acc.at[there, :], crawl_recv.at[c], cr_ss, cr_rs, p)
    crawl_recv[c] = crawl_acc[mine_rows, :]

    for t in range(max(quarters - 2, 0), quarters):
        pass_on(t)

    take(crawl_recv.at[pl.ds(0, nx - 1)], cr_rs)
    crawl_out[mine_rows, :] = summed(crawl_recv, nx)
    for p in x_peers:
        send(crawl_out.at[mine_rows, :], crawl_out.at[mine_rows, :], ca_ss, ca_rs, p)

    def place(y_, z_):
        return bench_out.at[pl.ds(pl.multiple_of(k * half + y_ * part + z_ * piece, piece), piece), :]

    def back(v, d, n):
        return lax.rem(v + n - d, n)

    take(zrecv.at[pl.ds(0, nz - 1)], fz_rs)
    place(y, z)[...] = summed(zrecv, nz)
    y_up, y_down = at(k, lax.rem(y + 1, YS), z), at(k, lax.rem(y + YS - 1, YS), z)
    z_up, z_down = at(k, y, lax.rem(z + 1, nz)), at(k, y, lax.rem(z + nz - 1, nz))
    ups = nz // 2

    def forward(d):
        got = place(y, back(z, d, nz))
        if d:
            take(got, gz_rs.at[d - 1])
        if d < ups:
            send(got, got, gz_ss, gz_rs.at[d], z_up)
        if d == 0 and nz > 2 or d > ups + 1:
            send(got, got, gz_ss, gz_rs.at[(d or nz) - 2], z_down)
        send(got, got, gy_ss, gy_rs.at[1, d], at(k, lax.rem(y + 2, YS), z))
        send(got, got, gy_ss, gy_rs.at[0, d], y_up)
        send(got, got, gy_ss, gy_rs.at[2, d], y_down)
        send(got, got, gc_ss, gc_rs, sibling)

    def relay(d):
        for e, p, first in ((1, y_up, 0), (3, y_down, 1)):
            y_, z_ = back(y, e, YS), back(z, d, nz)
            got = place(y_, z_)
            take(got, gy_rs.at[e - 1, d])
            send(got, got, gc_ss, gc_rs, sibling)

    def last(d):
        got = place(back(y, 2, YS), back(z, d, nz))
        take(got, gy_rs.at[1, d])
        send(got, got, gc_ss, gc_rs, sibling)

    order = sorted(range(nz), key=lambda d: min(d, nz - d))
    lags = (3, 6)
    for i in range(nz + lags[1]):
        if i < nz:
            forward(order[i])
        if 0 <= i - lags[0] < nz:
            relay(order[i - lags[0]])
        if 0 <= i - lags[1] < nz:
            last(order[i - lags[1]])

    take(crawl_recv.at[pl.ds(0, nx - 1)], ca_rs)
    take(crawl_recv.at[pl.ds(0, nx - 1)], ca_ss)
    take(crawl_recv.at[pl.ds(0, nx - 1)], cr_ss)
    take(bench_out.at[pl.ds(0, half), :], gc_rs)
    take(bench_out.at[pl.ds(0, half), :], gc_ss)
    take(bench_out.at[pl.ds(0, half - part), :], gy_ss)
    take(zrecv.at[pl.ds(0, nz - 1)], gz_ss)
    take(zrecv.at[pl.ds(0, nz - 1)], fz_ss)
    take(yrecv.at[:, pl.ds(0, YS - 1)], y_ss)
    take(sib, sib_ss)


def solution(mesh):
    nx = mesh.shape["cols"]
    nz = mesh.shape["rows"] // (CORES * YS)
    na = CORES * YS

    def per_device(crawl, bench, start_duals, row_cotangent, col_cotangent):
        rows, depth = crawl.shape
        cols = bench.shape[0]
        half, part = cols // CORES, cols // (CORES * YS)
        vmem, dma = pltpu.VMEM, pltpu.SemaphoreType.DMA
        scratch = [
            vmem((rows, depth), jnp.bfloat16), vmem((cols, depth), jnp.bfloat16),
            vmem((1, cols), F32), vmem((1, rows), F32), vmem((1, cols), F32), dma((5,)),
            vmem((rows, cols), F32),
            vmem((depth, rows), jnp.bfloat16),
            vmem((rows, 128), F32),
            vmem((rows, 128), F32),
            vmem((rows, 128), F32),
            vmem((rows, 128), F32),
            vmem((8, cols), F32), vmem((1, rows), F32),
            *[vmem((1, cols), F32)] * 5,
            vmem((2, rows), F32), vmem((nx, 2, rows), F32),
            vmem((3, 1, rows), F32), vmem((3, nx, 1, rows), F32),
            vmem((CORES, 2, half), F32), vmem((na, 2, half), F32),
            vmem((2, CORES, 1, half), F32), vmem((2, na, 1, half), F32),
            vmem((2, half), F32), vmem((nz, 2, half), F32),
            vmem((2, 1, half), F32), vmem((2, nz, 1, half), F32),
            vmem((3, CORES, 1, half), F32),
            vmem((rows, depth), F32), vmem((nx, rows // nx, depth), F32),
            vmem((part // 128, depth, YS * 128), F32), vmem((part // 128, depth, YS * 128), F32),
            vmem((part // 128, depth, YS * 128), F32), vmem((part // 128, YS, depth, 128), F32),
            vmem((part, depth), F32), vmem((nz, part // nz, depth), F32),
            dma((4, 2)), dma((4, 2)), dma((3,)), dma((3,)), dma((3,)), dma((3,)), dma((3,)), dma((3,)),
            dma, dma, dma, dma,
            dma, dma((part // 128,)), dma, dma((part // 128,)), dma, dma,
            dma, dma((nz - 1,)), dma, dma((YS - 1, nz)), dma, dma,
        ]
        return pl.pallas_call(
            functools.partial(kernel, nx, nz),
            out_shape=(vmem((rows, depth), F32), vmem((cols, depth), F32)),
            in_specs=[pl.BlockSpec(memory_space=pltpu.HBM)] * 5,
            out_specs=(pl.BlockSpec(memory_space=vmem),) * 2,
            scratch_shapes=scratch,
            compiler_params=pltpu.CompilerParams(
                collective_id=0, has_side_effects=True, vmem_limit_bytes=56 << 20
            ),
        )(crawl, bench, start_duals[None, :], row_cotangent[None, :], col_cotangent[None, :])

    placed = (P("rows", None), P("cols", None), P("cols"), P("rows"), P("cols"))
    return jax.shard_map(
        per_device,
        mesh=mesh,
        in_specs=placed,
        out_specs=(P("rows", None), P("cols", None)),
        check_vma=False,
    )
```

```python
import functools
import math

import jax
import jax.numpy as jnp
from jax import lax
from jax.experimental import pallas as pl
from jax.experimental.pallas import tpu as pltpu
from jax.sharding import PartitionSpec as P

EPSILON = 0.05
SCALE = math.log2(math.e) / EPSILON
MESH = pl.DeviceIdType.MESH
F32 = jnp.float32
CORES, YS = 2, 4


def kernel(
    nx, nz,
    crawl_in, bench_in, start_in, row_cot_in, col_cot_in,
    crawl_out, bench_out,
    crawl, bench, start, row_cot, col_cot, in_s, tile, crawl_t, lane_max, alpha_b, beta_b, back_b,
    kept, rowvec, colmax, fvec, gvec, avec, bvec,
    xs1, xr1, xs, xr, as1, ar1, as_, ar, zs1, zr1, zs, zr, cg,
    crawl_acc, crawl_recv, bench_part, sib, ysend, yrecv, zpart, zrecv,
    x_ss, x_rs, a_ss, a_rs, z_ss, z_rs, g_ss, g_rs,
    cr_ss, cr_rs, ca_ss, ca_rs, sib_ss, sib_rs, y_ss, y_rs, fz_ss, fz_rs,
    gz_ss, gz_rs, gy_ss, gy_rs, gc_ss, gc_rs,
):
    rows, depth = crawl.shape
    cols = bench.shape[0]
    half, part = cols // CORES, cols // (CORES * YS)
    na = CORES * YS
    r, c = lax.axis_index("rows"), lax.axis_index("cols")
    k, y, z = lax.rem(r, CORES), lax.rem(lax.div(r, CORES), YS), lax.div(r, na)
    a = lax.rem(r, na)

    def at(k_, y_, z_):
        return ((z_ * YS + y_) * CORES + k_, c)

    x_peers = [(r, lax.rem(c + d, nx)) for d in sorted(range(1, nx), key=lambda d: -min(d, nx - d))]
    a_peers = []
    for d in (4, 5, 3, 2, 6, 7, 1):
        o = lax.rem(a + d, na)
        a_peers.append((lax.rem(o, CORES), at(lax.rem(o, CORES), lax.div(o, CORES), z)))
    by_far = sorted(range(1, nz), key=lambda d: -min(d, nz - d))
    z_peers = [(lax.rem(z + d, nz), at(k, y, lax.rem(z + d, nz))) for d in by_far]
    sibling = at(1 - k, y, z)

    loads = [
        pltpu.make_async_copy(src, dst, in_s.at[i])
        for i, (src, dst) in enumerate((
            (crawl_in, crawl), (bench_in, bench), (start_in, start), (row_cot_in, row_cot), (col_cot_in, col_cot),
        ))
    ]
    for load in loads:
        load.start()

    barrier = pltpu.get_barrier_semaphore()
    everyone = x_peers + [p for _, p in a_peers] + [p for _, p in z_peers]
    for p in everyone:
        pl.semaphore_signal(barrier, inc=1, device_id=p, device_id_type=MESH)

    def send(src, dst, ss, rs, p):
        pltpu.make_async_remote_copy(
            src_ref=src, dst_ref=dst, send_sem=ss, recv_sem=rs, device_id=p, device_id_type=MESH
        ).start()

    def take(ref, sem):
        pltpu.make_async_copy(ref, ref, sem).wait()

    hr = rows // 2
    halves = [slice(h * hr, (h + 1) * hr) for h in range(2)]

    def x_send(n, h, src, recv):
        s = halves[h]
        for p in x_peers:
            send(src.at[:, s], recv.at[c, :, s], x_ss.at[n, h], x_rs.at[n, h], p)
        recv[c, :, s] = src[:, s]

    def x_take(n, h, recv):
        others = recv.at[pl.ds(0, nx - 1), :, halves[h]]
        take(others, x_rs.at[n, h])
        take(others, x_ss.at[n, h])

    def a_exchange(n, src, recv):
        for o, p in a_peers:
            send(src.at[o], recv.at[a], a_ss.at[n], a_rs.at[n], p)
        recv[a] = src[k]
        others = recv.at[pl.ds(0, na - 1)]
        take(others, a_rs.at[n])
        take(others, a_ss.at[n])

    def z_exchange(n, src, recv):
        for _, p in z_peers:
            send(src, recv.at[z], z_ss.at[n], z_rs.at[n], p)
        recv[z] = src[...]
        others = recv.at[pl.ds(0, nz - 1)]
        take(others, z_rs.at[n])
        take(others, z_ss.at[n])

    def core_gather(n, value):
        cg[n, k] = value
        send(cg.at[n, k], cg.at[n, k], g_ss.at[n], g_rs.at[n], sibling)
        take(cg.at[n, k], g_rs.at[n])
        take(cg.at[n, k], g_ss.at[n])

    def summed(recv, n, s=slice(None)):
        total = recv[0, :, s]
        for i in range(1, n):
            total = total + recv[i, :, s]
        return total

    def combined(recv, n, s=slice(None)):
        top = recv[0, 0:1, s]
        for i in range(1, n):
            top = jnp.maximum(top, recv[i, 0:1, s])
        total = recv[0, 1:2, s] * jnp.exp2(recv[0, 0:1, s] - top)
        for i in range(1, n):
            total = total + recv[i, 1:2, s] * jnp.exp2(recv[i, 0:1, s] - top)
        return top, total

    def spread(vec, out, h):
        for i in range(hr // 128):
            piece = vec[:, i * 128 : (i + 1) * 128]
            o = h * hr + i * 128
            out[o : o + 128, :] = jnp.broadcast_to(piece, (128, 128)).T

    def row_pass(d, n):
        out = xs.at[n]

        def step(i, carry):
            base = pl.multiple_of(i * 128, 128)
            pieces = []
            for h in range(2):
                acc = jnp.zeros((64, 128), F32)
                for j in range(cols // 128):
                    s = slice(j * 128, (j + 1) * 128)
                    acc = acc + tile[pl.ds(base + h * 64, 64), s] * d[0:1, s]
                pieces.append(acc)
            acc = jnp.concatenate(pieces, 0).T
            out[0:1, pl.ds(base, 128)] = jnp.sum(acc, 0, keepdims=True)
            return carry

        for h in range(2):
            lax.fori_loop(h * (hr // 128), (h + 1) * (hr // 128), step, 0, unroll=2)
            x_send(n + 1, h, out, xr.at[n])

    width = min(1024, cols)

    def col_loop(h, init, step, keep, finish):
        for cb in range(cols // width):
            at_ = [slice(cb * width + j * 128, cb * width + (j + 1) * 128) for j in range(width // 128)]
            first = tuple(jnp.full((8, 128), init, F32) if h == 0 else keep[:, s] for s in at_)
            last_ = lax.fori_loop(
                h * (hr // 64), (h + 1) * (hr // 64), lambda i, accs, at_=at_: step(i, accs, at_), first, unroll=2
            )
            for s, acc in zip(at_, last_):
                if h == 0:
                    keep[:, s] = acc
                else:
                    finish(s, acc)

    def col_pass(w, ready, finish):
        def step(i, accs, at_):
            base = pl.multiple_of(i * 64, 64)
            wb = w[pl.ds(base, 64), :]
            return tuple(
                acc + jnp.sum((tile[pl.ds(base, 64), s] * wb).reshape(8, 8, 128), 0) for acc, s in zip(accs, at_)
            )

        for h in range(2):
            ready(h)
            col_loop(h, 0.0, step, kept, lambda s, acc: finish(s.start, jnp.sum(acc, 0, keepdims=True)))

    for load in loads:
        load.wait()
    crawl_t[...] = crawl[...].astype(F32).T.astype(jnp.bfloat16)
    lane_max[...] = jnp.full(lane_max.shape, -jnp.inf, F32)
    mm = min(512, cols)
    rb = min(256, rows)

    def score_step(t, carry):
        i, jb = lax.rem(t, rows // rb), lax.div(t, rows // rb)
        base = pl.multiple_of(i * rb, rb)
        off = pl.multiple_of(jb * mm, mm)
        s = lax.dot_general(
            crawl[pl.ds(base, rb), :], bench[pl.ds(off, mm), :], (((1,), (1,)), ((), ())),
            preferred_element_type=F32,
        )
        s = s * SCALE + start[0:1, pl.ds(off, mm)] * SCALE
        tile[pl.ds(base, rb), pl.ds(off, mm)] = s
        top = lane_max[pl.ds(base, rb), :]
        for j in range(mm // 128):
            top = jnp.maximum(top, s[:, j * 128 : (j + 1) * 128])
        lane_max[pl.ds(base, rb), :] = top
        return carry

    lax.fori_loop(0, (rows // rb) * (cols // mm), score_step, 0, unroll=8)

    def level_step(i, carry):
        base = pl.multiple_of(i * 128, 128)
        tops, sums = [], []
        for h in range(2):
            at_ = pl.ds(base + h * 64, 64)
            top = lane_max[at_, :]
            acc = jnp.zeros((64, 128), F32)
            for j in range(cols // 128):
                acc = acc + jnp.exp2(tile[at_, j * 128 : (j + 1) * 128] - top)
            tops.append(top)
            sums.append(acc)
        top = jnp.concatenate(tops, 0).T
        acc = jnp.concatenate(sums, 0).T
        best = jnp.max(top, 0, keepdims=True)
        xs1[0:1, pl.ds(base, 128)] = best
        xs1[1:2, pl.ds(base, 128)] = jnp.sum(acc * jnp.exp2(top - best), 0, keepdims=True)
        return carry

    for h in range(2):
        lax.fori_loop(h * (hr // 128), (h + 1) * (hr // 128), level_step, 0)
        if h == 0:
            pl.semaphore_wait(barrier, len(everyone))
        x_send(0, h, xs1, xr1)

    def top_step(i, tops, at_):
        base = pl.multiple_of(i * 64, 64)
        lev = alpha_b[pl.ds(base, 64), :]
        return tuple(
            jnp.maximum(top, jnp.max((tile[pl.ds(base, 64), s] - lev).reshape(8, 8, 128), 0))
            for top, s in zip(tops, at_)
        )

    def top_finish(s, top):
        colmax[0:1, s] = jnp.max(top, 0, keepdims=True)

    for h in range(2):
        x_take(0, h, xr1)
        top, total = combined(xr1, nx, halves[h])
        spread(top + jnp.log2(total), alpha_b, h)
        col_loop(h, -jnp.inf, top_step, kept, top_finish)

    for cb in range(cols // width):
        def exp_step(i, accs, cb=cb):
            base = pl.multiple_of(i * 64, 64)
            lev = alpha_b[pl.ds(base, 64), :]
            new = []
            for j in range(width // 128):
                o = cb * width + j * 128
                e = jnp.exp2((tile[pl.ds(base, 64), o : o + 128] - lev) - colmax[0:1, o : o + 128])
                tile[pl.ds(base, 64), o : o + 128] = e
                new.append(accs[j] + jnp.sum(e.reshape(8, 8, 128), 0))
            return tuple(new)

        accs = lax.fori_loop(
            0, rows // 64, exp_step, tuple(jnp.zeros((8, 128), F32) for _ in range(width // 128))
        )
        for j in range(width // 128):
            o = cb * width + j * 128
            h, p = o // half, o % half
            as1[h, 0:1, p : p + 128] = colmax[0:1, o : o + 128]
            as1[h, 1:2, p : p + 128] = jnp.sum(accs[j], 0, keepdims=True)
    gvec[...] = jnp.exp2(colmax[...])

    a_exchange(0, as1, ar1)
    top, total = combined(ar1, na)
    zs1[0:1, :] = top
    zs1[1:2, :] = total
    z_exchange(0, zs1, zr1)
    top, total = combined(zr1, nz)
    core_gather(0, top + jnp.log2(total))
    for h in range(CORES):
        s = slice(h * half, (h + 1) * half)
        fvec[0:1, s] = jnp.exp2(colmax[0:1, s] - cg[0, h])

    row_pass(fvec, 0)

    def alpha_ready(h):
        x_take(1, h, xr.at[0])
        alpha = 1.0 / summed(xr.at[0], nx, halves[h])
        rowvec[:, halves[h]] = alpha
        spread(alpha, alpha_b, h)

    def col_reduce(n, w, ready):
        def finish(o, v):
            h, p = o // half, o % half
            as_[n, h, 0:1, p : p + 128] = v * fvec[0:1, o : o + 128]

        col_pass(w, ready, finish)
        a_exchange(n + 1, as_.at[n], ar.at[n])
        zs[n] = summed(ar.at[n], na)
        z_exchange(n + 1, zs.at[n], zr.at[n])
        core_gather(n + 1, summed(zr.at[n], nz))

    col_reduce(0, alpha_b, alpha_ready)
    for h in range(CORES):
        s = slice(h * half, (h + 1) * half)
        avec[0:1, s] = fvec[0:1, s] * col_cot[0:1, s] / cg[1, h]

    row_pass(avec, 1)

    def beta_ready(h):
        x_take(2, h, xr.at[1])
        alpha = rowvec[:, halves[h]]
        back2 = row_cot[:, halves[h]] - alpha * summed(xr.at[1], nx, halves[h])
        spread(back2 * alpha, beta_b, h)

    col_reduce(1, beta_b, beta_ready)
    for h in range(CORES):
        s = slice(h * half, (h + 1) * half)
        bvec[0:1, s] = -fvec[0:1, s] * cg[2, h]

    row_pass(bvec, 2)
    for h in range(2):
        x_take(3, h, xr.at[2])
        spread(-summed(xr.at[2], nx, halves[h]), back_b, h)

    crawl_acc[...] = jnp.zeros(crawl_acc.shape, F32)

    def grad_chunk(core, q, out):
        offs = [pl.multiple_of(core * half + o * part + q * 128, 128) for o in range(YS)]
        some_bench = jnp.concatenate([bench[pl.ds(o, 128), :] for o in offs], 0)
        acc = None
        for i in range(rows // rb):
            blocks = []
            for h in range(rb // 64):
                at_ = slice(i * rb + h * 64, i * rb + (h + 1) * 64)
                al, be, ba = alpha_b[at_, :], beta_b[at_, :], back_b[at_, :]
                pieces = []
                for o in offs:
                    s = pl.ds(o, 128)
                    bracket = (al * avec[0:1, s] + be * fvec[0:1, s]) + (bvec[0:1, s] + ba * gvec[0:1, s])
                    pieces.append((-(tile[at_, s] * bracket)).astype(jnp.bfloat16))
                blocks.append(jnp.concatenate(pieces, 1))
            grads = jnp.concatenate(blocks, 0)
            at_ = slice(i * rb, (i + 1) * rb)
            crawl_acc[at_, :] += jnp.dot(grads, some_bench, preferred_element_type=F32)
            product = jnp.dot(crawl_t[:, at_], grads, preferred_element_type=F32)
            acc = product if acc is None else acc + product
        out[...] = acc

    piece = part // nz
    quarters = part // 128
    per = nz // quarters

    def quarter(t):
        u = quarters - 1 - t
        if quarters == 4:
            u = u + lax.div(u, 2) * (1 - 2 * lax.rem(u, 2))
        return lax.rem(lax.div(z, per) + u, quarters)

    def pass_on(t):
        q = quarter(t)
        take(yrecv.at[t, pl.ds(0, YS - 1)], y_rs.at[t])
        total = yrecv[t, 0]
        for i in range(1, YS):
            total = total + yrecv[t, i]
        zpart[pl.ds(pl.multiple_of(q * 128, 128), 128), :] = total.T
        for i in range(per):
            o = q * per + i
            src = zpart.at[pl.ds(pl.multiple_of(o * piece, piece), piece), :]

            @pl.when(o != z)
            def _(o=o, src=src):
                send(src, zrecv.at[z], fz_ss, fz_rs, at(k, y, o))

            @pl.when(o == z)
            def _(o=o, src=src):
                zrecv[z] = src[...]

    def gradient_step(t, carry):
        q = quarter(t)
        grad_chunk(1 - k, q, bench_part.at[t])
        send(bench_part.at[t], sib.at[t], sib_ss, sib_rs.at[t], sibling)
        grad_chunk(k, q, ysend.at[t])
        take(sib.at[t], sib_rs.at[t])
        for o in range(YS):
            s = slice(o * 128, (o + 1) * 128)
            ysend[t, :, s] = ysend[t, :, s] + sib[t, :, s]

            @pl.when(o != y)
            def _(o=o, s=s):
                send(ysend.at[t, :, s], yrecv.at[t, y], y_ss, y_rs.at[t], at(k, o, z))

            @pl.when(o == y)
            def _(o=o, s=s):
                yrecv[t, y] = ysend[t, :, s]

        @pl.when(t >= 2)
        def _():
            pass_on(t - 2)

        return carry

    lax.fori_loop(0, quarters, gradient_step, 0)

    quarter_rows = rows // nx
    mine_rows = pl.ds(pl.multiple_of(c * quarter_rows, quarter_rows), quarter_rows)
    for p in x_peers:
        there = pl.ds(pl.multiple_of(p[1] * quarter_rows, quarter_rows), quarter_rows)
        send(crawl_acc.at[there, :], crawl_recv.at[c], cr_ss, cr_rs, p)
    crawl_recv[c] = crawl_acc[mine_rows, :]

    for t in range(max(quarters - 2, 0), quarters):
        pass_on(t)

    take(crawl_recv.at[pl.ds(0, nx - 1)], cr_rs)
    crawl_out[mine_rows, :] = summed(crawl_recv, nx)
    for p in x_peers:
        send(crawl_out.at[mine_rows, :], crawl_out.at[mine_rows, :], ca_ss, ca_rs, p)

    def place(y_, z_):
        return bench_out.at[pl.ds(pl.multiple_of(k * half + y_ * part + z_ * piece, piece), piece), :]

    def back(v, d, n):
        return lax.rem(v + n - d, n)

    take(zrecv.at[pl.ds(0, nz - 1)], fz_rs)
    place(y, z)[...] = summed(zrecv, nz)
    y_up, y_down = at(k, lax.rem(y + 1, YS), z), at(k, lax.rem(y + YS - 1, YS), z)
    z_up, z_down = at(k, y, lax.rem(z + 1, nz)), at(k, y, lax.rem(z + nz - 1, nz))
    ups = nz // 2

    def forward(d):
        got = place(y, back(z, d, nz))
        if d:
            take(got, gz_rs.at[d - 1])
        if d < ups:
            send(got, got, gz_ss, gz_rs.at[d], z_up)
        if d == 0 and nz > 2 or d > ups + 1:
            send(got, got, gz_ss, gz_rs.at[(d or nz) - 2], z_down)
        send(got, got, gy_ss, gy_rs.at[1, d], at(k, lax.rem(y + 2, YS), z))
        send(got, got, gy_ss, gy_rs.at[0, d], y_up)
        send(got, got, gy_ss, gy_rs.at[2, d], y_down)
        send(got, got, gc_ss, gc_rs, sibling)

    def relay(d):
        for e, p, first in ((1, y_up, 0), (3, y_down, 1)):
            y_, z_ = back(y, e, YS), back(z, d, nz)
            got = place(y_, z_)
            take(got, gy_rs.at[e - 1, d])
            send(got, got, gc_ss, gc_rs, sibling)

    def last(d):
        got = place(back(y, 2, YS), back(z, d, nz))
        take(got, gy_rs.at[1, d])
        send(got, got, gc_ss, gc_rs, sibling)

    order = sorted(range(nz), key=lambda d: min(d, nz - d))
    lags = (3, 6)
    for i in range(nz + lags[1]):
        if i < nz:
            forward(order[i])
        if 0 <= i - lags[0] < nz:
            relay(order[i - lags[0]])
        if 0 <= i - lags[1] < nz:
            last(order[i - lags[1]])

    take(crawl_recv.at[pl.ds(0, nx - 1)], ca_rs)
    take(crawl_recv.at[pl.ds(0, nx - 1)], ca_ss)
    take(crawl_recv.at[pl.ds(0, nx - 1)], cr_ss)
    take(bench_out.at[pl.ds(0, half), :], gc_rs)
    take(bench_out.at[pl.ds(0, half), :], gc_ss)
    take(bench_out.at[pl.ds(0, half - part), :], gy_ss)
    take(zrecv.at[pl.ds(0, nz - 1)], gz_ss)
    take(zrecv.at[pl.ds(0, nz - 1)], fz_ss)
    take(yrecv.at[:, pl.ds(0, YS - 1)], y_ss)
    take(sib, sib_ss)


def solution(mesh):
    nx = mesh.shape["cols"]
    nz = mesh.shape["rows"] // (CORES * YS)
    na = CORES * YS

    def per_device(crawl, bench, start_duals, row_cotangent, col_cotangent):
        rows, depth = crawl.shape
        cols = bench.shape[0]
        half, part = cols // CORES, cols // (CORES * YS)
        vmem, dma = pltpu.VMEM, pltpu.SemaphoreType.DMA
        scratch = [
            vmem((rows, depth), jnp.bfloat16), vmem((cols, depth), jnp.bfloat16),
            vmem((1, cols), F32), vmem((1, rows), F32), vmem((1, cols), F32), dma((5,)),
            vmem((rows, cols), F32),
            vmem((depth, rows), jnp.bfloat16),
            vmem((rows, 128), F32),
            vmem((rows, 128), F32),
            vmem((rows, 128), F32),
            vmem((rows, 128), F32),
            vmem((8, cols), F32), vmem((1, rows), F32),
            *[vmem((1, cols), F32)] * 5,
            vmem((2, rows), F32), vmem((nx, 2, rows), F32),
            vmem((3, 1, rows), F32), vmem((3, nx, 1, rows), F32),
            vmem((CORES, 2, half), F32), vmem((na, 2, half), F32),
            vmem((2, CORES, 1, half), F32), vmem((2, na, 1, half), F32),
            vmem((2, half), F32), vmem((nz, 2, half), F32),
            vmem((2, 1, half), F32), vmem((2, nz, 1, half), F32),
            vmem((3, CORES, 1, half), F32),
            vmem((rows, depth), F32), vmem((nx, rows // nx, depth), F32),
            vmem((part // 128, depth, YS * 128), F32), vmem((part // 128, depth, YS * 128), F32),
            vmem((part // 128, depth, YS * 128), F32), vmem((part // 128, YS, depth, 128), F32),
            vmem((part, depth), F32), vmem((nz, part // nz, depth), F32),
            dma((4, 2)), dma((4, 2)), dma((3,)), dma((3,)), dma((3,)), dma((3,)), dma((3,)), dma((3,)),
            dma, dma, dma, dma,
            dma, dma((part // 128,)), dma, dma((part // 128,)), dma, dma,
            dma, dma((nz - 1,)), dma, dma((YS - 1, nz)), dma, dma,
        ]
        return pl.pallas_call(
            functools.partial(kernel, nx, nz),
            out_shape=(vmem((rows, depth), F32), vmem((cols, depth), F32)),
            in_specs=[pl.BlockSpec(memory_space=pltpu.HBM)] * 5,
            out_specs=(pl.BlockSpec(memory_space=vmem),) * 2,
            scratch_shapes=scratch,
            compiler_params=pltpu.CompilerParams(
                collective_id=0, has_side_effects=True, vmem_limit_bytes=56 << 20
            ),
        )(crawl, bench, start_duals[None, :], row_cotangent[None, :], col_cotangent[None, :])

    placed = (P("rows", None), P("cols", None), P("cols"), P("rows"), P("cols"))
    return jax.shard_map(
        per_device,
        mesh=mesh,
        in_specs=placed,
        out_specs=(P("rows", None), P("cols", None)),
        check_vma=False,
    )
```
